256 devices in a mesh: market: 32 (over z, y), sub: 8 (over x, core).
Axes of the slice: x: 4, y: 4, z: 8, core: 2. Of those that a mesh axis runs over, the one named last changes fastest.
Arguments:
- buyers: float32 [32768, 512], P(('market', 'sub'))
- sellers: float32 [32768, 512], P(('market', 'sub'))
- eligibility: int32 [32, 32], replicated, may hold values from 0 to 1, as said below
- positives: int32 [32768], P(('market', 'sub')), may hold values from 0 to 32767, as said below
Outputs:
- buyer_grad: float32 [32768, 512], P(('market', 'sub'))
- seller_grad: float32 [32768, 512], P(('market', 'sub'))
- loss: float32 [], replicated
The draws below stay inside these ranges and needn't reach their ends.
Inputs may be any that keep to these rules, and one draw needn't show every extreme that they name: eligibility[g, g] = 1 for every group; every row has 1 to 16 ones, and some row has exactly 16. positives[i] lies in the same market group as i, and every seller index appears exactly once.
All inputs are finite; a program needn't handle non-finite values.
Results may differ from the reference program's by a relative error of at most 0.0038.
The reference program's roundings to bfloat16 on the way count: a program that leaves them out, or rounds other values in their place, can miss the bound.
Values may be sent and summed in bfloat16 or wider, within the bound.
A program may use at most 64 MiB of HBM per device.

```python
import math
import jax
import jax.numpy as jnp
from jax import lax

EMBED = 512
ROWS_DEV = 128
GROUP_ROWS = 1024
GROUPS = 32
BATCH = 32768
ELIG = 16


def shared_rows(key):
    key_sign, key_level = jax.random.split(key)
    signs = jnp.where(jax.random.bernoulli(key_sign, 0.5, (BATCH, EMBED)), 1.0, -1.0)
    level = jax.random.randint(key_level, (BATCH, 1), 0, 3).astype(jnp.float32)
    return signs * (2.4 + 0.4 * level)


def row_roles():
    local = jnp.arange(BATCH) % ROWS_DEV
    first_rows = (local == 2) | (local == ROWS_DEV // 2)
    second_rows = (local == 3) | (local == ROWS_DEV // 2 + 1)
    return (first_rows[:, None], second_rows[:, None])


def tower_draw(key, shared, sign_term):
    key_base, key_scale = jax.random.split(key, 2)
    base = jnp.clip(jax.random.normal(key_base, (BATCH, EMBED), jnp.float32), -4.0, 4.0)
    scales = jnp.exp(jax.random.uniform(key_scale, (BATCH, 1), jnp.float32, math.log(0.3), math.log(3.0)))
    values = base * scales
    alternate = 1.0 - 2.0 * (jnp.arange(EMBED) % 2).astype(jnp.float32)
    previous = jnp.roll(shared, 1, axis=0)
    first_rows, second_rows = row_roles()
    values = jnp.where(first_rows, shared, values)
    values = jnp.where(second_rows, 0.99 * previous + sign_term * previous * alternate, values)
    return values


def draw_buyers(key, part):
    shared = shared_rows(key)
    key = jax.random.fold_in(key, 11)
    return tower_draw(key, shared, -0.5)


def draw_sellers(key, part):
    shared = shared_rows(key)
    key = jax.random.fold_in(key, 12)
    return tower_draw(key, shared, 0.5)


def draw_eligibility(key, part):
    key = jax.random.fold_in(key, 21)
    key_score, key_first, key_second, key_busy = jax.random.split(key, 4)
    column_ids = jnp.arange(GROUPS, dtype=jnp.int32)
    scores = jax.random.randint(key_score, (GROUPS, GROUPS), 0, 1024) * GROUPS + column_ids[None, :]
    scores = jnp.where(column_ids[:, None] == column_ids[None, :], 4096 * GROUPS, scores)
    ranking = jnp.argsort(jnp.argsort(-scores, axis=1, stable=True), axis=1, stable=True)
    counts = jnp.minimum(jax.random.randint(key_first, (GROUPS,), 1, ELIG + 1), jax.random.randint(key_second, (GROUPS,), 1, ELIG + 1))
    busiest = jax.random.randint(key_busy, (), 0, GROUPS)
    counts = jnp.where(column_ids == busiest, ELIG, counts)
    return (ranking < counts[:, None]).astype(jnp.int32)


def draw_positives(key, part):
    key = jax.random.fold_in(key, 31)
    group_keys = jax.random.split(key, GROUPS)
    shuffles = jax.vmap(lambda single: jax.random.permutation(single, GROUP_ROWS))(group_keys)
    offsets = jnp.arange(GROUPS, dtype=jnp.int32)[:, None] * GROUP_ROWS
    return (offsets + shuffles.astype(jnp.int32)).reshape(BATCH).astype(jnp.int32)


def setup_inputs(seed: int = 0) -> dict:
    streams_of = jax.random.split(jax.random.key(seed), 5)
    return {
        "buyers": draw_buyers(jax.random.fold_in(streams_of[4], 71), 0),
        "sellers": draw_sellers(jax.random.fold_in(streams_of[4], 71), 0),
        "eligibility": draw_eligibility(jax.random.fold_in(streams_of[4], 71), 0),
        "positives": draw_positives(jax.random.fold_in(streams_of[4], 71), 0),
    }


neg_fill = -1e+30

def reference(buyers, sellers, eligibility, positives):
    logit_scale = 1.0 / math.sqrt(EMBED)
    buyer_half = buyers.astype(jnp.bfloat16)
    seller_half = sellers.astype(jnp.bfloat16)
    col_ids = jnp.arange(BATCH, dtype=jnp.int32)
    col_group = (col_ids // GROUP_ROWS).astype(jnp.int32)

    def logits(group_idx):
        row_block = lax.dynamic_slice_in_dim(buyer_half, group_idx * GROUP_ROWS, GROUP_ROWS, 0)
        scores = jnp.dot(row_block, seller_half.T, preferred_element_type=jnp.float32) * logit_scale
        allowed = jnp.take(eligibility[group_idx], col_group) > 0
        pos_block = lax.dynamic_slice_in_dim(positives, group_idx * GROUP_ROWS, GROUP_ROWS, 0)
        is_hit = col_ids[None, :] == pos_block[:, None]
        return (row_block, scores, allowed[None, :], is_hit)

    def first_pass(totals, group_idx):
        col_max, col_sum = totals
        row_block, scores, allowed, is_hit = logits(group_idx)
        masked = jnp.where(allowed, scores, neg_fill)
        top_row = lax.optimization_barrier(jnp.max(masked, axis=1))
        row_sum = lax.optimization_barrier(jnp.sum(jnp.where(allowed, jnp.exp(scores - top_row[:, None]), 0.0), axis=1))
        pos_logits = lax.optimization_barrier(jnp.sum(jnp.where(is_hit, scores, 0.0), axis=1))
        new_max = jnp.maximum(col_max, lax.optimization_barrier(jnp.max(masked, axis=0)))
        new_sum = col_sum * jnp.exp(col_max - new_max) + lax.optimization_barrier(jnp.sum(jnp.where(allowed, jnp.exp(scores - new_max[None, :]), 0.0), axis=0))
        return ((new_max, new_sum), (top_row + jnp.log(row_sum), pos_logits))
    start_state = (jnp.full((BATCH,), neg_fill, jnp.float32), jnp.zeros((BATCH,), jnp.float32))
    (col_max, col_sum), (row_lse, pos_logits) = lax.scan(first_pass, start_state, jnp.arange(GROUPS, dtype=jnp.int32))
    row_lse = row_lse.reshape(BATCH)
    col_lse = col_max + jnp.log(col_sum)
    loss = (jnp.sum(row_lse) + jnp.sum(col_lse) - 2.0 * jnp.sum(pos_logits)) / (2.0 * BATCH)

    def second_pass(seller_acc, group_idx):
        row_block, scores, allowed, is_hit = logits(group_idx)
        block_lse = lax.dynamic_slice_in_dim(row_lse, group_idx * GROUP_ROWS, GROUP_ROWS, 0)
        prob_row = jnp.where(allowed, jnp.exp(scores - block_lse[:, None]), 0.0)
        prob_col = jnp.where(allowed, jnp.exp(scores - col_lse[None, :]), 0.0)
        weights_half = (0.5 * (prob_row + prob_col) - jnp.where(is_hit, 1.0, 0.0)).astype(jnp.bfloat16)
        buyer_block = jnp.dot(weights_half, seller_half, preferred_element_type=jnp.float32)
        seller_acc = seller_acc + jnp.dot(weights_half.T, row_block, preferred_element_type=jnp.float32)
        return (seller_acc, buyer_block)
    seller_grad, buyer_grad = lax.scan(second_pass, jnp.zeros((BATCH, EMBED), jnp.float32), jnp.arange(GROUPS, dtype=jnp.int32))
    return (buyer_grad.reshape(BATCH, EMBED), seller_grad, loss)
```

```python
import math

import jax
import jax.numpy as jnp
from jax import lax
from jax.experimental import pallas as pl
from jax.experimental.pallas import tpu as pltpu
from jax.sharding import PartitionSpec as P

neg_fill = -1e30
MESH = pl.DeviceIdType.MESH
NZ, NY, NX, NC = 8, 4, 4, 2
ROWS = 128
EMBED = 512
LOG2E = 1.0 / math.log(2.0)
SLOTS = 16
F32 = jnp.float32
BF16 = jnp.bfloat16


def mod(value, size):
    return lax.rem(value + size, size)


def as_row(column, eye):
    return jnp.sum(jnp.where(eye, column, 0.0), axis=0, keepdims=True)


def as_column(row, eye):
    return jnp.sum(jnp.where(eye, row, 0.0), axis=1, keepdims=True)


def kernel(
    buyers_ref, sellers_ref, elig_ref, pos_ref,
    bgrad_ref, sgrad_ref, loss_ref,
    b_all, s_all, bt_all, score, pbuf, qbuf,
    pos_f, pos_cols, row_stat, col_stat, row_send, row_recv, col_send, col_recv,
    rowl_send, rowl_recv, coll_send, coll_recv, loss_recv, rl_cols,
    sib_s, sib_r, z_s, z_r, f0_s, f0_r, f1_s, f1_r, mid, g0_s, g0_r, g1_s, g1_r, seller_t,
    next_ref, slot_ref, list_ref,
    send_sem, recv_sem, st_send, st_recv,
):
    market = lax.axis_index("market")
    sub = lax.axis_index("sub")
    z, y = lax.div(market, NY), lax.rem(market, NY)
    x, c = lax.div(sub, NC), lax.rem(sub, NC)
    other = 1 - c
    row_id = z * NC + c
    col_id = y * NX + x

    def dev(zz, yy, xx, cc):
        return (zz * NY + yy, xx * NC + cc)

    def zdev(step):
        return dev(mod(z + step, NZ), y, x, c)

    def ydev(step):
        return dev(z, mod(y + step, NY), x, c)

    def xdev(step):
        return dev(z, y, mod(x + step, NX), c)

    sibling = dev(z, y, x, other)

    def line_dev(place):
        return dev(lax.div(place, NC), y, x, lax.rem(place, NC))

    def plane_dev(place):
        return dev(z, lax.div(place, NX), lax.rem(place, NX), c)

    barrier = pltpu.get_barrier_semaphore()

    def greet(step, carry):
        pl.semaphore_signal(
            barrier, inc=1, device_id=line_dev(mod(row_id + step, 16)), device_id_type=MESH
        )
        pl.semaphore_signal(
            barrier, inc=1, device_id=plane_dev(mod(col_id + step, 16)), device_id_type=MESH
        )
        return carry

    lax.fori_loop(1, 16, greet, 0)
    b_all[z, c] = buyers_ref[...].astype(BF16)
    s_all[y, x] = sellers_ref[...].astype(BF16)
    own_pos = pos_ref[...] - market * (ROWS * NX * NC)
    pos_f[c] = jnp.broadcast_to(own_pos.astype(F32), (8, ROWS))
    pl.semaphore_wait(barrier, 30)

    names = {}
    pending = []

    def sem_of(name):
        return names.setdefault(name, len(names))

    def send(name, src, dst, device):
        place = sem_of(name)
        copy = pltpu.make_async_remote_copy(
            src_ref=src, dst_ref=dst, send_sem=send_sem.at[place], recv_sem=recv_sem.at[place],
            device_id=device, device_id_type=MESH,
        )
        copy.start()
        pending.append(copy)

    def arrive(name, dst):
        place = sem_of(name)
        pltpu.make_async_remote_copy(
            src_ref=dst, dst_ref=dst, send_sem=send_sem.at[place], recv_sem=recv_sem.at[place],
            device_id=sibling, device_id_type=MESH,
        ).wait_recv()

    def b_at(step, core, lo=0, rows=ROWS):
        return b_all.at[mod(z + step, NZ), core, pl.ds(lo, rows)]

    def s_at(first_axis, first_step, second_step, lo, rows):
        if first_axis == "x":
            return s_all.at[mod(y + second_step, NY), mod(x + first_step, NX), pl.ds(lo, rows)]
        return s_all.at[mod(y + first_step, NY), mod(x + second_step, NX), pl.ds(lo, rows)]

    halves = (("x", xdev, ydev, 0), ("y", ydev, xdev, 64))

    def send_second(axis, dev2, lo, step1):
        ref = s_at(axis, step1, 0, lo, 64)
        for sign in (1, -1):
            send(("s2", axis, step1, sign), ref, ref, dev2(sign))

    def relay_second(axis, dev2, lo, step1):
        for sign in (1, -1):
            arrive(("s2", axis, step1, sign), s_at(axis, step1, -sign, lo, 64))
            part = lo if sign == 1 else lo + 32
            ref = s_at(axis, step1, -sign, part, 32)
            send(("s3", axis, step1, sign), ref, ref, dev2(sign))

    def finish_second(axis, lo, step1):
        for sign in (1, -1):
            part = lo if sign == 1 else lo + 32
            arrive(("s3", axis, step1, sign), s_at(axis, step1, 2, part, 32))

    for sign in (1, -1):
        send(("b", 1, sign), b_at(0, c), b_at(0, c), zdev(sign))
    for axis, dev1, dev2, lo in halves:
        ref = s_at(axis, 0, 0, lo, 64)
        for sign in (1, -1):
            send(("s0", axis, sign), ref, ref, dev1(sign))
    for axis, dev1, dev2, lo in halves:
        send_second(axis, dev2, lo, 0)
    send(("pos",), pos_f.at[c], pos_f.at[c], sibling)
    send(("bs", 0), b_at(0, c), b_at(0, c), sibling)

    own_block = z * NY + y

    def walk_back(i, carry):
        following, count = carry
        block = NZ * NY - 1 - i
        flag = elig_ref[lax.div(block, NY) * NY + y, z * NY + lax.rem(block, NY)]
        next_ref[block] = following
        live = jnp.logical_and(flag > 0, block != own_block)
        return (jnp.where(live, block, following), count + jnp.where(live, 1, 0))

    first, count = lax.fori_loop(0, NZ * NY, walk_back, (own_block, 0))

    def rank(block, seen):
        flag = elig_ref[lax.div(block, NY) * NY + y, z * NY + lax.rem(block, NY)]
        live = jnp.logical_and(flag > 0, block != own_block)
        slot_ref[block] = jnp.where(
            block == own_block, 0, jnp.where(live, 1 + seen, SLOTS)
        )
        return seen + jnp.where(live, 1, 0)

    lax.fori_loop(0, NZ * NY, rank, 0)
    list_ref[0] = own_block

    def walk(t, block):
        list_ref[t] = block
        return next_ref[block]

    lax.fori_loop(1, SLOTS, walk, first)

    for sign in (1, -1):
        arrive(("b", 1, sign), b_at(-sign, c))
        send(("b", 2, sign), b_at(-sign, c), b_at(-sign, c), zdev(sign))
        send(("bs", -sign), b_at(-sign, c), b_at(-sign, c), sibling)
    for axis, dev1, dev2, lo in halves:
        for sign in (1, -1):
            arrive(("s0", axis, sign), s_at(axis, -sign, 0, lo, 64))
            part = lo if sign == 1 else lo + 32
            ref = s_at(axis, -sign, 0, part, 32)
            send(("s1", axis, sign), ref, ref, dev1(sign))
            send_second(axis, dev2, lo, -sign)
    for axis, dev1, dev2, lo in halves:
        relay_second(axis, dev2, lo, 0)
    for sign in (1, -1):
        arrive(("b", 2, sign), b_at(-2 * sign, c))
        send(("b", 3, sign), b_at(-2 * sign, c), b_at(-2 * sign, c), zdev(sign))
        send(("bs", -2 * sign), b_at(-2 * sign, c), b_at(-2 * sign, c), sibling)
    for axis, dev1, dev2, lo in halves:
        for sign in (1, -1):
            part = lo if sign == 1 else lo + 32
            arrive(("s1", axis, sign), s_at(axis, 2, 0, part, 32))
        send_second(axis, dev2, lo, 2)
    for axis, dev1, dev2, lo in halves:
        for step1 in (-1, 1):
            relay_second(axis, dev2, lo, step1)
    for sign in (1, -1):
        arrive(("b", 3, sign), b_at(-3 * sign, c))
        part = 0 if sign == 1 else 64
        ref = b_at(-3 * sign, c, part, 64)
        send(("b", 4, sign), ref, ref, zdev(sign))
        send(("bs", -3 * sign), b_at(-3 * sign, c), b_at(-3 * sign, c), sibling)
    for axis, dev1, dev2, lo in halves:
        relay_second(axis, dev2, lo, 2)
    for sign in (1, -1):
        part = 0 if sign == 1 else 64
        arrive(("b", 4, sign), b_at(4, c, part, 64))
    send(("bs", 4), b_at(4, c), b_at(4, c), sibling)
    for axis, dev1, dev2, lo in halves:
        for step1 in (0, -1, 1, 2):
            finish_second(axis, lo, step1)
    arrive(("pos",), pos_f.at[other])
    for step in (0, 1, -1, 2, -2, 3, -3, 4):
        arrive(("bs", step), b_at(step, other))

    eye = lax.broadcasted_iota(jnp.int32, (ROWS, ROWS), 0) == lax.broadcasted_iota(
        jnp.int32, (ROWS, ROWS), 1
    )
    unit = LOG2E / math.sqrt(EMBED)

    def transpose_buyers(zz, carry):
        bt_all[zz] = b_all[zz].reshape(NC * ROWS, EMBED).T
        return carry

    lax.fori_loop(0, NZ, transpose_buyers, 0)
    for core in range(NC):
        pos_cols[core * ROWS : (core + 1) * ROWS, :] = jnp.broadcast_to(
            as_column(pos_f[core, 0:1, :], eye), (ROWS, ROWS)
        )

    def hits(xx):
        lane = lax.broadcasted_iota(jnp.int32, (NC * ROWS, ROWS), 1) + (xx * NC + c) * ROWS
        return pos_cols[...] == lane.astype(F32)

    row_stat[SLOTS] = jnp.zeros(row_stat.shape[1:], F32)
    col_stat[SLOTS] = jnp.zeros(col_stat.shape[1:], F32)
    for core in range(NC):
        row_stat[SLOTS, core, 0:1, :] = jnp.full((1, ROWS), neg_fill, F32)
    for xx in range(NX):
        col_stat[SLOTS, xx, 0:1, :] = jnp.full((1, ROWS), neg_fill, F32)

    def first_pass(t, carry):
        block = list_ref[t]
        left = b_all[lax.div(block, NY)].reshape(NC * ROWS, EMBED)
        right = s_all[lax.rem(block, NY)].reshape(NX * ROWS, EMBED)
        tile = (
            lax.dot_general(left, right, (((1,), (1,)), ((), ())), preferred_element_type=F32)
            * unit
        )
        score[t] = tile
        row_top = jnp.max(tile, axis=1, keepdims=True)
        row_sum = jnp.sum(jnp.exp2(tile - row_top), axis=1, keepdims=True)
        col_top = jnp.max(tile, axis=0, keepdims=True)
        col_sum = jnp.sum(jnp.exp2(tile - col_top), axis=0, keepdims=True)
        for core in range(NC):
            span = slice(core * ROWS, (core + 1) * ROWS)
            row_stat[t, core, 0:1, :] = as_row(row_top[span], eye)
            row_stat[t, core, 1:2, :] = as_row(row_sum[span], eye)
        for xx in range(NX):
            span = slice(xx * ROWS, (xx + 1) * ROWS)
            col_stat[t, xx, 0:1, :] = col_top[:, span]
            col_stat[t, xx, 1:2, :] = col_sum[:, span]
        return carry

    lax.fori_loop(0, SLOTS, first_pass, 0)
    matched = jnp.zeros((NC * ROWS, 1), F32)
    for xx in range(NX):
        matched = matched + jnp.sum(
            jnp.where(hits(xx), score[0, :, xx * ROWS : (xx + 1) * ROWS], 0.0),
            axis=1, keepdims=True,
        )

    def merge(tops, sums):
        top = tops[0]
        for item in tops[1:]:
            top = jnp.maximum(top, item)
        total = jnp.zeros_like(top)
        for item, amount in zip(tops, sums):
            total = total + amount * jnp.exp2(item - top)
        return top, total

    row_send[...] = jnp.zeros(row_send.shape, F32)
    col_send[...] = jnp.zeros(col_send.shape, F32)
    for core in range(NC):
        row_send[z * NC + core, 2:3, :] = as_row(matched[core * ROWS : (core + 1) * ROWS], eye)

    def merge_rows(zz, carry):
        slots = [slot_ref[zz * NY + yy] for yy in range(NY)]
        for core in range(NC):
            top, total = merge(
                [row_stat[s, core, 0:1, :] for s in slots], [row_stat[s, core, 1:2, :] for s in slots]
            )
            row_send[zz * NC + core, 0:1, :] = top
            row_send[zz * NC + core, 1:2, :] = total
        return carry

    lax.fori_loop(0, NZ, merge_rows, 0)

    def merge_cols(yy, carry):
        slots = [slot_ref[zz * NY + yy] for zz in range(NZ)]
        for xx in range(NX):
            top, total = merge(
                [col_stat[s, xx, 0:1, :] for s in slots], [col_stat[s, xx, 1:2, :] for s in slots]
            )
            col_send[yy * NX + xx, 0:1, :] = top
            col_send[yy * NX + xx, 1:2, :] = total
        return carry

    lax.fori_loop(0, NY, merge_cols, 0)

    def small(kind, src, dst, step, device):
        return pltpu.make_async_remote_copy(
            src_ref=src, dst_ref=dst, send_sem=st_send.at[kind, step],
            recv_sem=st_recv.at[kind, step], device_id=device, device_id_type=MESH,
        )

    def scatter(step, carry):
        to = mod(row_id + step, 16)
        small(0, row_send.at[to], row_recv.at[row_id], step, line_dev(to)).start()
        to = mod(col_id + step, 16)
        small(1, col_send.at[to], col_recv.at[col_id], step, plane_dev(to)).start()
        return carry

    def scattered(step, carry):
        origin = mod(row_id - step, 16)
        small(0, row_send.at[origin], row_recv.at[origin], step, sibling).wait()
        origin = mod(col_id - step, 16)
        small(1, col_send.at[origin], col_recv.at[origin], step, sibling).wait()
        return carry

    lax.fori_loop(1, 16, scatter, 0)
    row_recv[row_id] = row_send[row_id]
    col_recv[col_id] = col_send[col_id]
    lax.fori_loop(1, 16, scattered, 0)

    def own_lse(recv):
        top, total = merge(
            [recv[i, 0:1, :] for i in range(16)], [recv[i, 1:2, :] for i in range(16)]
        )
        return top + jnp.log2(total)

    own_row, own_col = own_lse(row_recv), own_lse(col_recv)
    own_match = row_recv[0, 2:3, :]
    for i in range(1, 16):
        own_match = own_match + row_recv[i, 2:3, :]
    terms = jnp.sum(own_row + own_col - 2.0 * own_match, axis=1, keepdims=True)
    rowl_send[0:1, :] = own_row
    rowl_send[1:8, :] = jnp.broadcast_to(terms, (7, ROWS))
    coll_send[...] = jnp.broadcast_to(own_col, (8, ROWS))

    def spread(step, carry):
        to = mod(row_id + step, 16)
        small(2, rowl_send, rowl_recv.at[row_id], step, line_dev(to)).start()
        to = mod(col_id + step, 16)
        small(3, coll_send, coll_recv.at[col_id], step, plane_dev(to)).start()
        return carry

    def spreaded(step, carry):
        small(2, rowl_send, rowl_recv.at[mod(row_id - step, 16)], step, sibling).wait()
        small(3, coll_send, coll_recv.at[mod(col_id - step, 16)], step, sibling).wait()
        return carry

    lax.fori_loop(1, 16, spread, 0)
    rowl_recv[row_id] = rowl_send[...]
    coll_recv[col_id] = coll_send[...]
    lax.fori_loop(1, 16, spreaded, 0)

    line_terms = rowl_recv[0, 1:2, :]
    for i in range(1, 16):
        line_terms = line_terms + rowl_recv[i, 1:2, :]
    loss_recv[col_id] = jnp.broadcast_to(line_terms, (8, ROWS))

    def tell(step, carry):
        to = mod(col_id + step, 16)
        small(4, loss_recv.at[col_id], loss_recv.at[col_id], step, plane_dev(to)).start()
        return carry

    lax.fori_loop(1, 16, tell, 0)

    def spread_rows(zz, carry):
        for core in range(NC):
            rl_cols[zz, core * ROWS : (core + 1) * ROWS, :] = jnp.broadcast_to(
                as_column(rowl_recv[zz * NC + core, 0:1, :], eye) + 1.0, (ROWS, ROWS)
            )
        return carry

    lax.fori_loop(0, NZ, spread_rows, 0)

    def second_pass(t, own):
        block = list_ref[t]
        zz, yy = lax.div(block, NY), lax.rem(block, NY)
        row_lse = rl_cols[zz]
        parts = []
        for xx in range(NX):
            tile = score[t, :, xx * ROWS : (xx + 1) * ROWS]
            col_lse = coll_recv[yy * NX + xx, 0:1, :] + 1.0
            mixed = jnp.exp2(tile - row_lse) + jnp.exp2(tile - col_lse)
            if own:
                mixed = mixed - jnp.where(hits(xx), 1.0, 0.0)
            parts.append(mixed.astype(BF16))
        weights = jnp.concatenate(parts, axis=1)
        right = s_all[yy].reshape(NX * ROWS, EMBED)
        term = jnp.dot(weights, right, preferred_element_type=F32)
        for core in range(NC):
            pbuf[t, core] = term[core * ROWS : (core + 1) * ROWS]
        term = jnp.dot(bt_all[zz], weights, preferred_element_type=F32)
        for xx in range(NX):
            qbuf[t, xx] = term[:, xx * ROWS : (xx + 1) * ROWS]

    second_pass(0, True)

    def other_blocks(t, carry):
        second_pass(t, False)
        return carry

    lax.fori_loop(1, SLOTS, other_blocks, 0)
    pbuf[SLOTS] = jnp.zeros(pbuf.shape[1:], F32)
    qbuf[SLOTS] = jnp.zeros(qbuf.shape[1:], F32)

    step_rows = 32

    def by_rows(lo, rows, body):
        def at(i, carry):
            body(pl.multiple_of(lo + i * step_rows, step_rows))
            return carry

        lax.fori_loop(0, rows // step_rows, at, 0)

    def p_sum(zz, core, at):
        total = None
        for yy in range(NY):
            term = pbuf[slot_ref[zz * NY + yy], core, pl.ds(at, step_rows), :]
            total = term if total is None else total + term
        return total

    def q_sum(yy, xx, at):
        total = None
        for zz in range(NZ):
            term = qbuf[slot_ref[zz * NY + yy], xx, pl.ds(at, step_rows), :]
            total = term if total is None else total + term
        return total

    order = (4, 3, -3, 2, -2, 1, -1, 0)
    for place, step in enumerate(order):
        def fill(at, place=place, step=step):
            sib_s[place, pl.ds(at, step_rows), :] = p_sum(mod(z + step, NZ), other, at).astype(BF16)

        by_rows(0, ROWS, fill)
        send(("gs", place), sib_s.at[place], sib_r.at[place], sibling)

    grads = ((0, "y", ydev, xdev, 0), (1, "x", xdev, ydev, 256))

    def q_at(axis, step, lane, at):
        if axis == "y":
            return q_sum(mod(y + step, NY), lane, at)
        return q_sum(lane, mod(x + step, NX), at)

    for h, axis, dev1, dev2, base in grads:
        for d, sign in enumerate((1, -1)):
            for lane in range(4):
                def fill(at, h=h, axis=axis, d=d, lane=lane, base=base):
                    f0_s[h, d, lane, pl.ds(at, step_rows), :] = q_at(
                        axis, 2, lane, base + d * 128 + at
                    ).astype(BF16)

                by_rows(0, 128, fill)
            send(("f0", h, sign), f0_s.at[h, d], f0_r.at[h, d], dev1(sign))

    def z_value(place, step, at):
        return p_sum(mod(z + step, NZ), c, at) + sib_r[place, pl.ds(at, step_rows), :].astype(F32)

    def z_send(place, step, d, sign, hop, lo, rows):
        def fill(at):
            value = z_value(place, step, at)
            z_s[d, hop, pl.ds(at, step_rows), :] = value.astype(BF16)

        def fill_more(at):
            value = z_value(place, step, at)
            value = value + z_r[d, hop - 1, pl.ds(at, step_rows), :].astype(F32)
            z_s[d, hop, pl.ds(at, step_rows), :] = value.astype(BF16)

        if hop == 0:
            by_rows(lo, rows, fill)
        elif hop == 1:
            first_lo = d * 64
            arrive(("gz", 0, sign), z_r.at[d, 0, pl.ds(first_lo, 64)])
            by_rows(first_lo, 64, fill_more)
            by_rows(64 - first_lo, 64, fill)
        else:
            arrive(("gz", hop - 1, sign), z_r.at[d, hop - 1])
            by_rows(0, ROWS, fill_more)
        ref = z_s.at[d, hop, pl.ds(lo, rows)]
        send(("gz", hop, sign), ref, z_r.at[d, hop, pl.ds(lo, rows)], zdev(sign))

    arrive(("gs", 0), sib_r.at[0])
    z_send(0, 4, 0, 1, 0, 0, 64)
    z_send(0, 4, 1, -1, 0, 64, 64)

    for h, axis, dev1, dev2, base in grads:
        for d, sign in enumerate((1, -1)):
            for lane in range(4):
                def fill(at, h=h, axis=axis, d=d, sign=sign, lane=lane, base=base):
                    f1_s[h, d, lane, pl.ds(at, step_rows), :] = q_at(
                        axis, sign, lane, base + at
                    ).astype(BF16)

                def fill_more(at, h=h, axis=axis, d=d, sign=sign, lane=lane, base=base):
                    value = q_at(axis, sign, lane, base + d * 128 + at)
                    value = value + f0_r[h, d, lane, pl.ds(at, step_rows), :].astype(F32)
                    f1_s[h, d, lane, pl.ds(d * 128 + at, step_rows), :] = value.astype(BF16)

                by_rows(128 - d * 128, 128, fill)
                if lane == 0:
                    arrive(("f0", h, sign), f0_r.at[h, d])
                by_rows(0, 128, fill_more)
            send(("f1", h, sign), f1_s.at[h, d], f1_r.at[h, d], dev1(sign))

    arrive(("gs", 1), sib_r.at[1])
    z_send(1, 3, 0, 1, 1, 0, ROWS)
    arrive(("gs", 2), sib_r.at[2])
    z_send(2, -3, 1, -1, 1, 0, ROWS)

    for h, axis, dev1, dev2, base in grads:
        for lane in range(4):
            def own_fill(at, h=h, axis=axis, lane=lane, base=base):
                mid[h, lane, pl.ds(at, step_rows), :] = q_at(axis, 0, lane, base + at)

            by_rows(0, 256, own_fill)
    arrive(("gs", 3), sib_r.at[3])
    z_send(3, 2, 0, 1, 2, 0, ROWS)
    arrive(("gs", 4), sib_r.at[4])
    z_send(4, -2, 1, -1, 2, 0, ROWS)

    for h, axis, dev1, dev2, base in grads:
        for d, sign in enumerate((1, -1)):
            arrive(("f1", h, sign), f1_r.at[h, d])
        for lane in range(4):
            def own_add(at, h=h, lane=lane):
                span = pl.ds(at, step_rows)
                mid[h, lane, span, :] = (
                    mid[h, lane, span, :]
                    + f1_r[h, 0, lane, span, :].astype(F32)
                    + f1_r[h, 1, lane, span, :].astype(F32)
                )

            by_rows(0, 256, own_add)
        place = x if axis == "y" else y
        far = mod(place + 2, 4)
        for d, sign in enumerate((1, -1)):
            g0_s[h, d] = mid[h, far, d * 128 : (d + 1) * 128, :].astype(BF16)
            send(("g0", h, sign), g0_s.at[h, d], g0_r.at[h, d], dev2(sign))
    for h, axis, dev1, dev2, base in grads:
        place = x if axis == "y" else y
        for d, sign in enumerate((1, -1)):
            near = mod(place + sign, 4)
            arrive(("g0", h, sign), g0_r.at[h, d])
            own_lo = 128 - d * 128
            g1_s[h, d, own_lo : own_lo + 128, :] = mid[
                h, near, own_lo : own_lo + 128, :
            ].astype(BF16)
            g1_s[h, d, d * 128 : (d + 1) * 128, :] = (
                mid[h, near, d * 128 : (d + 1) * 128, :] + g0_r[h, d].astype(F32)
            ).astype(BF16)
            send(("g1", h, sign), g1_s.at[h, d], g1_r.at[h, d], dev2(sign))

    arrive(("gs", 5), sib_r.at[5])
    z_send(5, 1, 0, 1, 3, 0, ROWS)
    arrive(("gs", 6), sib_r.at[6])
    z_send(6, -1, 1, -1, 3, 0, ROWS)

    for h, axis, dev1, dev2, base in grads:
        place = x if axis == "y" else y
        for d, sign in enumerate((1, -1)):
            arrive(("g1", h, sign), g1_r.at[h, d])
        seller_t[h * 256 : (h + 1) * 256, :] = (
            mid[h, place] + g1_r[h, 0].astype(F32) + g1_r[h, 1].astype(F32)
        )
    sgrad_ref[...] = seller_t[...].T

    arrive(("gs", 7), sib_r.at[7])
    for d, sign in enumerate((1, -1)):
        arrive(("gz", 3, sign), z_r.at[d, 3])

    def finish(at):
        span = pl.ds(at, step_rows)
        bgrad_ref[span, :] = (
            z_value(7, 0, at) + z_r[0, 3, span, :].astype(F32) + z_r[1, 3, span, :].astype(F32)
        )

    by_rows(0, ROWS, finish)

    def told(step, carry):
        small(
            4, loss_recv.at[col_id], loss_recv.at[mod(col_id - step, 16)], step, sibling
        ).wait()
        return carry

    lax.fori_loop(1, 16, told, 0)
    total = loss_recv[0, 0:1, :]
    for i in range(1, 16):
        total = total + loss_recv[i, 0:1, :]
    loss_ref[...] = total * (math.log(2.0) / (2.0 * ROWS * NZ * NY * NX * NC))
    for copy in pending:
        copy.wait_send()


def vmem(shape, dtype):
    return pltpu.VMEM(shape, dtype)


def fast(buyers, sellers, eligibility, positives):
    scratch = [
        vmem((NZ, NC, ROWS, EMBED), BF16),
        vmem((NY, NX, ROWS, EMBED), BF16),
        vmem((NZ, EMBED, NC * ROWS), BF16),
        vmem((SLOTS, NC * ROWS, NX * ROWS), F32),
        vmem((SLOTS + 1, NC, ROWS, EMBED), F32),
        vmem((SLOTS + 1, NX, EMBED, ROWS), F32),
        vmem((NC, 8, ROWS), F32),
        vmem((NC * ROWS, ROWS), F32),
        vmem((SLOTS + 1, NC, 8, ROWS), F32),
        vmem((SLOTS + 1, NX, 8, ROWS), F32),
        vmem((16, 8, ROWS), F32),
        vmem((16, 8, ROWS), F32),
        vmem((16, 8, ROWS), F32),
        vmem((16, 8, ROWS), F32),
        vmem((8, ROWS), F32),
        vmem((16, 8, ROWS), F32),
        vmem((8, ROWS), F32),
        vmem((16, 8, ROWS), F32),
        vmem((16, 8, ROWS), F32),
        vmem((NZ, NC * ROWS, ROWS), F32),
        vmem((NZ, ROWS, EMBED), BF16),
        vmem((NZ, ROWS, EMBED), BF16),
        vmem((2, 4, ROWS, EMBED), BF16),
        vmem((2, 4, ROWS, EMBED), BF16),
        vmem((2, 2, 4, 128, ROWS), BF16),
        vmem((2, 2, 4, 128, ROWS), BF16),
        vmem((2, 2, 4, 256, ROWS), BF16),
        vmem((2, 2, 4, 256, ROWS), BF16),
        vmem((2, 4, 256, ROWS), F32),
        vmem((2, 2, 128, ROWS), BF16),
        vmem((2, 2, 128, ROWS), BF16),
        vmem((2, 2, 256, ROWS), BF16),
        vmem((2, 2, 256, ROWS), BF16),
        vmem((EMBED, ROWS), F32),
        pltpu.SMEM((NZ * NY,), jnp.int32),
        pltpu.SMEM((NZ * NY,), jnp.int32),
        pltpu.SMEM((SLOTS,), jnp.int32),
        pltpu.SemaphoreType.DMA((96,)),
        pltpu.SemaphoreType.DMA((96,)),
        pltpu.SemaphoreType.DMA((5, 16)),
        pltpu.SemaphoreType.DMA((5, 16)),
    ]
    in_vmem = pl.BlockSpec(memory_space=pltpu.VMEM)
    buyer_grad, seller_grad, loss = pl.pallas_call(
        kernel,
        out_shape=(
            jax.ShapeDtypeStruct((ROWS, EMBED), F32),
            jax.ShapeDtypeStruct((ROWS, EMBED), F32),
            jax.ShapeDtypeStruct((1, ROWS), F32),
        ),
        in_specs=[in_vmem, in_vmem, pl.BlockSpec(memory_space=pltpu.SMEM), in_vmem],
        out_specs=(in_vmem, in_vmem, in_vmem),
        scratch_shapes=scratch,
        compiler_params=pltpu.CompilerParams(
            collective_id=0, has_side_effects=True, vmem_limit_bytes=60 * 1024 * 1024
        ),
        name="two_tower",
    )(buyers, sellers, eligibility, positives.reshape(1, ROWS))
    return (buyer_grad, seller_grad, loss[0, 0])


def merged(part, axis, combine):
    gathered = jax.tree.map(lambda a: lax.all_gather(a, axis), part)

    def take(source):
        return jax.tree.map(lambda a: lax.dynamic_index_in_dim(a, source, 0, False), gathered)

    return lax.fori_loop(
        1, lax.axis_size(axis), lambda source, state: combine(state, take(source)), take(0)
    )


def tile_scores(left, right, factor):
    return (
        lax.dot_general(left, right, (((1,), (1,)), ((), ())), preferred_element_type=jnp.float32)
        * factor
    )


def row_combine(first_part, second_part):
    top = jnp.maximum(first_part[0], second_part[0])
    total = first_part[1] * jnp.exp(first_part[0] - top) + second_part[1] * jnp.exp(
        second_part[0] - top
    )
    return (top, total, first_part[2] + second_part[2])


def col_combine(first_part, second_part):
    top = jnp.maximum(first_part[0], second_part[0])
    total = first_part[1] * jnp.exp(first_part[0] - top) + second_part[1] * jnp.exp(
        second_part[0] - top
    )
    return (top, total)


def coefficient(scores, row_lse, col_lse, is_hit):
    mixed = 0.5 * (jnp.exp(scores - row_lse) + jnp.exp(scores - col_lse)) - jnp.where(
        is_hit, 1.0, 0.0
    )
    return mixed.astype(jnp.bfloat16)


def sweep_groups(stats_step, totals, flags, group_count):

    def outer(state, block_idx):
        outputs = []
        for offset in range(4):
            target = block_idx * 4 + offset
            state, result = stats_step(state, target, flags[target] > 0)
            outputs.append(result)
        stacked = jax.tree.map(lambda *items: jnp.stack(items), *outputs)
        return (state, stacked)

    return lax.scan(outer, totals, jnp.arange(group_count // 4))


def general(buyers, sellers, eligibility, positives):
    row_count, embed_width = buyers.shape
    sub_count = lax.axis_size("sub")
    group_count = lax.axis_size("market")
    group_rows = row_count * sub_count
    market_pos = lax.axis_index("market")
    sub_pos = lax.axis_index("sub")
    factor = 1.0 / math.sqrt(embed_width)
    local_cols = jnp.arange(row_count, dtype=jnp.int32)
    buyer_half = buyers.astype(jnp.bfloat16)
    seller_half = sellers.astype(jnp.bfloat16)
    group_buyers, group_pos = (
        lax.all_gather(buyer_half, "sub", axis=0, tiled=True),
        lax.all_gather(positives, "sub", axis=0, tiled=True),
    )
    seller_panel = lax.all_gather(seller_half, "market", axis=0, tiled=True)
    own_row = lax.dynamic_index_in_dim(eligibility, market_pos, 0, keepdims=False)

    def panel_block(target):
        return lax.dynamic_slice_in_dim(seller_panel, target * row_count, row_count, 0)

    def stats_step(state, target, is_live):
        row_max, row_sum = state

        def stats_live_branch(unused):
            scores = tile_scores(group_buyers, panel_block(target), factor)
            new_max = jnp.maximum(row_max, jnp.max(scores, axis=1))
            new_sum = row_sum * jnp.exp(row_max - new_max) + jnp.sum(
                jnp.exp(scores - new_max[:, None]), axis=1
            )
            col_top = jnp.max(scores, axis=0)
            col_total = jnp.sum(jnp.exp(scores - col_top[None, :]), axis=0)
            return ((new_max, new_sum), (col_top, col_total))

        def stats_dead_branch(unused):
            return (
                (row_max, row_sum),
                (
                    jnp.full((row_count,), neg_fill, jnp.float32),
                    jnp.zeros((row_count,), jnp.float32),
                ),
            )

        return lax.cond(is_live, stats_live_branch, stats_dead_branch, None)

    start_state = (
        jnp.full((group_rows,), neg_fill, jnp.float32),
        jnp.zeros((group_rows,), jnp.float32),
    )
    (row_max, row_sum), (col_top, col_total) = sweep_groups(
        stats_step, start_state, own_row, group_count
    )
    col_top = col_top.reshape(group_count * row_count)
    col_total = col_total.reshape(group_count * row_count)
    own_scores = tile_scores(group_buyers, seller_half, factor)
    own_ids = (market_pos * sub_count + sub_pos) * row_count + local_cols
    pos_part = jnp.sum(jnp.where(group_pos[:, None] == own_ids[None, :], own_scores, 0.0), axis=1)
    row_max, row_sum, pos_logits = merged((row_max, row_sum, pos_part), "sub", row_combine)
    col_top, col_total = merged((col_top, col_total), "market", col_combine)
    row_lse = row_max + jnp.log(row_sum)
    col_lse = col_top + jnp.log(col_total)
    row_own = lax.dynamic_slice_in_dim(row_lse, sub_pos * row_count, row_count, 0)
    col_own = lax.dynamic_slice_in_dim(col_lse, market_pos * row_count, row_count, 0)
    pos_own = lax.dynamic_slice_in_dim(pos_logits, sub_pos * row_count, row_count, 0)
    local_loss = jnp.sum(row_own) + jnp.sum(col_own) - 2.0 * jnp.sum(pos_own)
    total_loss = lax.psum(local_loss, ("market", "sub"))
    loss = total_loss / (2.0 * group_rows * group_count)

    def grad_step(state, target, is_live):

        def grad_live_branch(acc):
            block = panel_block(target)
            scores = tile_scores(group_buyers, block, factor)
            block_lse = lax.dynamic_slice_in_dim(col_lse, target * row_count, row_count, 0)
            block_ids = (target * sub_count + sub_pos) * row_count + local_cols
            weights_half = coefficient(
                scores,
                row_lse[:, None],
                block_lse[None, :],
                group_pos[:, None] == block_ids[None, :],
            )
            return acc + jnp.dot(weights_half, block, preferred_element_type=jnp.float32)

        return (lax.cond(is_live, grad_live_branch, lambda acc: acc, state), None)

    acc, unused = sweep_groups(
        grad_step,
        jnp.zeros((lax.axis_size("sub") * row_count, embed_width), jnp.float32),
        own_row,
        group_count,
    )
    buyer_grad = lax.psum_scatter(acc, "sub", scatter_dimension=0, tiled=True)
    row_span = lax.axis_size("market") * row_count

    def one_group(offset):

        def one_live_branch(unused):
            block = panel_block(offset)
            scores = tile_scores(group_buyers, block, factor)
            block_lse = lax.dynamic_slice_in_dim(col_lse, offset * row_count, row_count, 0)
            block_ids = (offset * sub_count + sub_pos) * row_count + local_cols
            weights_half = coefficient(
                scores,
                row_lse[:, None],
                block_lse[None, :],
                group_pos[:, None] == block_ids[None, :],
            )
            return lax.dot_general(
                weights_half,
                group_buyers,
                (((0,), (0,)), ((), ())),
                preferred_element_type=jnp.float32,
            )

        def one_dead_branch(unused):
            return jnp.zeros((row_count, embed_width), jnp.float32)

        return lax.cond(own_row[offset] > 0, one_live_branch, one_dead_branch, None)

    pieces = lax.map(one_group, jnp.arange(row_span // row_count))
    seller_grad = lax.psum_scatter(
        pieces.reshape(row_span, embed_width), "market", scatter_dimension=0, tiled=True
    )
    return (buyer_grad, seller_grad, loss)


def shards(buyers, sellers, eligibility, positives):
    blocks = (eligibility > 0).astype(jnp.int32).reshape(NZ, NY, NZ, NY)
    busiest = jnp.max(jnp.sum(blocks, axis=(0, 3)))
    return lax.cond(busiest <= SLOTS, fast, general, buyers, sellers, eligibility, positives)


def solution(mesh):
    return jax.shard_map(
        shards,
        mesh=mesh,
        in_specs=(
            P(("market", "sub"), None),
            P(("market", "sub"), None),
            P(),
            P(("market", "sub")),
        ),
        out_specs=(P(("market", "sub"), None), P(("market", "sub"), None), P()),
        check_vma=False,
    )
```

```python
import functools
import math

import jax
import jax.numpy as jnp
from jax import lax
from jax.experimental import pallas as pl
from jax.experimental.pallas import tpu as pltpu
from jax.sharding import PartitionSpec as P

neg_fill = -1e30
MESH = pl.DeviceIdType.MESH
NZ, NY, NX, NC = 8, 4, 4, 2
ROWS = 128
EMBED = 512
LOG2E = 1.0 / math.log(2.0)
SLOTS = 14
F32 = jnp.float32
BF16 = jnp.bfloat16


GATHER_ORDER = (
    ("b", 0, -1, 0), ("s0", 0, -1), ("bs", 0), ("b", 0, 1, 0), ("s0", 0, 1), ("s0", 1, 1), ("s2", 1, 0, 1),
    ("s0", 1, -1), ("b", 0, -1, 2), ("b", 0, 1, 1), ("b", 0, -1, 1), ("b", 0, 1, 2), ("s2", 0, 0, -1),
    ("s2", 0, 0, 1), ("s2", 1, 0, -1), ("b", 1, -1, 0), ("s2", 0, 1, 1), ("b", 1, 1, 0), ("s2", 1, -1, 1),
    ("s2", 0, 1, -1), ("s1", 0, -1), ("s1", 1, -1), ("b", 1, -1, 1), ("b", 1, 1, 1), ("b", 1, -1, 2),
    ("s1", 1, 1), ("s1", 0, 1), ("b", 1, 1, 2), ("s3", 0, 0, -1), ("s2", 1, 1, -1), ("s2", 1, 1, 1),
    ("s2", 1, -1, -1), ("s2", 0, -1, 1), ("s3", 0, 1, 1), ("b", 2, -1, 0), ("b", 2, 1, 1), ("s2", 0, -1, -1),
    ("b", 2, -1, 1), ("b", 2, 1, 0), ("s2", 1, 2, 1), ("b", 2, -1, 2), ("s2", 1, 2, -1), ("b", 2, 1, 2),
    ("s2", 0, 2, -1), ("s4", 0, 0, -1), ("bs", 2), ("s2", 0, 2, 1), ("bs", 1), ("bs", -2), ("s3", 1, 0, 1),
    ("s3", 1, -1, 1), ("s4", 0, 1, 1), ("b", 3, 1, 1), ("b", 3, -1, 0), ("s3", 1, 1, -1), ("b", 3, 1, 0),
    ("b", 3, -1, 1), ("s3", 0, -1, 1), ("s3", 1, -1, -1), ("s3", 0, 1, -1), ("s3", 1, 0, -1), ("s3", 1, 1, 1),
    ("bs", -1), ("s3", 0, 0, 1), ("s3", 1, 2, 1), ("s3", 0, -1, -1), ("bs", 3), ("s3", 1, 2, -1),
    ("s3", 0, 2, -1), ("s3", 0, 2, 1), ("bs", -3), ("bs", 4), ("s4", 1, 0, 1), ("s4", 1, 1, -1),
    ("s4", 0, -1, 1), ("s4", 1, 0, -1), ("s4", 0, -1, -1), ("s4", 1, -1, -1), ("s4", 1, -1, 1),
    ("s4", 1, 1, 1), ("s4", 0, 2, 1), ("s4", 0, 1, -1), ("s4", 0, 0, 1), ("s4", 0, 2, -1), ("s4", 1, 2, 1),
    ("s4", 1, 2, -1),
)
RETURN_ORDER = (
    ("f0", 1, 1, 0), ("sib", 0), ("f0", 1, 0, 0), ("f0", 0, 0, 0), ("f0", 0, 1, 2), ("sib", 4),
    ("f0", 1, 1, 2), ("f0", 1, 0, 1), ("f0", 0, 1, 0), ("fa", 1, 0, 2), ("sib", 2), ("f0", 0, 0, 1),
    ("f0", 1, 0, 2), ("loss", 0), ("f0", 1, 1, 1), ("fa", 0, 1, 0), ("sib", 1), ("z", 0, 0, 0),
    ("z", 1, 0, 3), ("sib", 7), ("z", 0, 0, 1), ("fa", 1, 1, 0), ("f0", 0, 0, 2), ("f0", 0, 1, 1),
    ("z", 1, 0, 2), ("sib", 5), ("z", 0, 1, 3), ("sib", 3), ("fb", 0, 0, 0), ("z", 1, 1, 0), ("fa", 0, 0, 0),
    ("fb", 1, 1, 0), ("fb", 1, 0, 0), ("fa", 1, 1, 1), ("loss", 1), ("fa", 0, 1, 1), ("z", 0, 1, 2),
    ("z", 1, 1, 1), ("fb", 0, 1, 0), ("fa", 1, 0, 0), ("z", 1, 1, 3), ("z", 0, 1, 0), ("fa", 1, 1, 2),
    ("fa", 0, 0, 1), ("fa", 1, 0, 1), ("z", 0, 1, 1), ("fb", 0, 0, 1), ("z", 1, 1, 2), ("z", 0, 2, 3),
    ("fb", 0, 1, 1), ("z", 1, 2, 0), ("sib", 6), ("fb", 1, 1, 1), ("fb", 1, 0, 1), ("z", 1, 2, 1),
    ("z", 0, 2, 2), ("mid", 1, 0), ("loss", 2), ("z", 0, 2, 0), ("g0", 1, 1), ("g0", 1, 0), ("z", 1, 2, 3),
    ("mid", 0, 0), ("g0", 0, 1), ("z", 1, 2, 2), ("g0", 0, 0), ("z", 0, 2, 1), ("fb", 0, 1, 2),
    ("fb", 0, 0, 2), ("fb", 1, 1, 2), ("fb", 1, 0, 2), ("fa", 0, 1, 2), ("fa", 0, 0, 2), ("z", 1, 3, 0),
    ("z", 0, 3, 3), ("z", 1, 3, 1), ("z", 0, 3, 2), ("mid", 1, 1), ("g1", 1, 1), ("g1", 1, 0), ("z", 0, 3, 0),
    ("z", 1, 3, 3), ("mid", 0, 1), ("loss", 3), ("g1", 0, 0), ("g1", 0, 1), ("z", 0, 3, 1), ("z", 1, 3, 2),
    ("mid", 0, 2), ("mid", 1, 2), ("gend", 1), ("zend",), ("gend", 0),
)


def mod(value, size):
    return lax.rem(value + size, size)


def as_row(column, eye):
    return jnp.sum(jnp.where(eye, column, 0.0), axis=0, keepdims=True)


def as_column(row, eye):
    return jnp.sum(jnp.where(eye, row, 0.0), axis=1, keepdims=True)


def kernel(
    dense,
    buyers_ref, sellers_ref, elig_ref, pos_ref,
    bgrad_ref, sgrad_ref, loss_ref,
    b_all, s_all, bt_all, score, pbuf, qbuf,
    pos_f, pos_cols, row_stat, col_stat, row_x, row_in, col_x, col_in,
    row_lse, col_lse, sum_x, sum_in, rl_cols,
    sib_s, sib_r, z_s, z_r, f0_s, f0_r, f1_s, f1_r, mid, g0_s, g0_r, g1_s, g1_r, seller_t,
    next_ref, slot_ref, list_ref,
    send_sem, recv_sem,
):
    slots = NZ * NY if dense else score.shape[0]
    market = lax.axis_index("market")
    sub = lax.axis_index("sub")
    z, y = lax.div(market, NY), lax.rem(market, NY)
    x, c = lax.div(sub, NC), lax.rem(sub, NC)
    other = 1 - c

    def dev(zz, yy, xx, cc):
        return (zz * NY + yy, xx * NC + cc)

    def zdev(step):
        return dev(mod(z + step, NZ), y, x, c)

    def ydev(step):
        return dev(z, mod(y + step, NY), x, c)

    def xdev(step):
        return dev(z, y, mod(x + step, NX), c)

    sibling = dev(z, y, x, other)

    row_peers = (
        sibling,
        dev(z + 1 - 2 * lax.rem(z, 2), y, x, c),
        dev(z + 2 - 4 * lax.rem(lax.div(z, 2), 2), y, x, c),
        dev(mod(z + 4, NZ), y, x, c),
    )
    col_peers = (
        dev(z, y, x + 1 - 2 * lax.rem(x, 2), c),
        dev(z, y, mod(x + 2, NX), c),
        dev(z, y + 1 - 2 * lax.rem(y, 2), x, c),
        dev(z, mod(y + 2, NY), x, c),
    )

    barrier = pltpu.get_barrier_semaphore()
    row_steps = [(dz, dc) for dz in (4, 3, 5, 2, 6, 1, 7, 0) for dc in (0, 1) if dz or dc]
    col_steps = [(dy, dx) for dy in (2, 1, 3, 0) for dx in (2, 1, 3, 0) if dy or dx]

    def core_of(dc):
        return other if dc else c

    for (dz, dc), (dy, dx) in zip(row_steps, col_steps):
        for peer in (
            dev(mod(z + dz, NZ), y, x, core_of(dc)),
            dev(z, mod(y + dy, NY), mod(x + dx, NX), c),
        ):
            pl.semaphore_signal(barrier, inc=1, device_id=peer, device_id_type=MESH)
    b_all[z, c] = buyers_ref[...].astype(BF16)
    s_all[y, x] = sellers_ref[...].astype(BF16)
    own_pos = pos_ref[...] - market * (ROWS * NX * NC)
    pos_f[c] = jnp.broadcast_to(own_pos.astype(F32), (8, ROWS))
    pl.semaphore_wait(barrier, 30)

    names = {}
    landed = set()
    pending = []

    def sem_of(name):
        return names.setdefault(name, len(names))

    def send(name, src, dst, device):
        place = sem_of(name)
        copy = pltpu.make_async_remote_copy(
            src_ref=src, dst_ref=dst, send_sem=send_sem.at[place], recv_sem=recv_sem.at[place],
            device_id=device, device_id_type=MESH,
        )
        copy.start()
        pending.append(copy)

    def arrive(name, dst):
        place = sem_of(name)
        pltpu.make_async_remote_copy(
            src_ref=dst, dst_ref=dst, send_sem=send_sem.at[place], recv_sem=recv_sem.at[place],
            device_id=sibling, device_id_type=MESH,
        ).wait_recv()

    def need(name, dst):
        if name not in landed:
            landed.add(name)
            arrive(name, dst)

    def b_at(step, core, lo=0, rows=ROWS):
        return b_all.at[mod(z + step, NZ), core, pl.ds(lo, rows)]

    def s_at(first_axis, first_step, second_step, lo, rows):
        if first_axis == "x":
            return s_all.at[mod(y + second_step, NY), mod(x + first_step, NX), pl.ds(lo, rows)]
        return s_all.at[mod(y + first_step, NY), mod(x + second_step, NX), pl.ds(lo, rows)]

    halves = (("x", xdev, ydev, 0), ("y", ydev, xdev, 64))

    z_parts = {1: ((0, 32), (32, 32), (64, 64)), -1: ((96, 32), (64, 32), (0, 64))}

    def z_ref(hop, sign, i):
        lo, rows = z_parts[sign][i]
        return b_at(-hop * sign, c, lo, rows)

    def have(step):
        if abs(step) == 4:
            wanted = [(4, sign, i) for sign in (1, -1) for i in range(2)]
        else:
            wanted = [(abs(step), -1 if step > 0 else 1, i) for i in range(3)] if step else []
        for hop, sign, i in wanted:
            need(("b", hop, sign, i), z_ref(hop, sign, i))

    def s_ref(kind, h, step1, sign):
        axis, dev1, dev2, lo = halves[h]
        part = lo if sign == 1 else lo + 32
        if kind == "s0":
            return s_at(axis, -sign, 0, lo, 64)
        if kind == "s1":
            return s_at(axis, 2, 0, part, 32)
        if kind == "s2":
            return s_at(axis, step1, -sign, lo, 64)
        return s_at(axis, step1, 2, part, 32)

    def gather_step(kind, *key):
        if kind == "b":
            hop, sign, i = key
            ref = z_ref(hop, sign, i)
            if hop:
                need(("b", hop, sign, i), ref)
            send(("b", hop + 1, sign, i), ref, ref, zdev(sign))
        elif kind == "bs":
            step = key[0]
            have(step)
            send(("bs", step), b_at(step, c), b_at(step, c), sibling)
        elif kind == "s0" or kind == "s1":
            h, sign = key
            axis, dev1, dev2, lo = halves[h]
            if kind == "s0":
                ref = s_at(axis, 0, 0, lo, 64)
            else:
                need(("s0", h, sign), s_ref("s0", h, 0, sign))
                ref = s_at(axis, -sign, 0, lo if sign == 1 else lo + 32, 32)
            send((kind, h, sign), ref, ref, dev1(sign))
        else:
            h, step1, sign = key
            axis, dev1, dev2, lo = halves[h]
            if kind == "s2":
                if abs(step1) == 1:
                    need(("s0", h, -step1), s_ref("s0", h, 0, -step1))
                elif step1 == 2:
                    for way in (1, -1):
                        need(("s1", h, way), s_ref("s1", h, 0, way))
                ref = s_at(axis, step1, 0, lo, 64)
            elif kind == "s3":
                need(("s2", h, step1, sign), s_ref("s2", h, step1, sign))
                ref = s_at(axis, step1, -sign, lo if sign == 1 else lo + 32, 32)
            else:
                need(("s3", h, step1, sign), s_ref("s3", h, step1, sign))
                return
            send((kind, h, step1, sign), ref, ref, dev2(sign))

    early = 8
    for task in GATHER_ORDER[:early]:
        gather_step(*task)
    send(("pos",), pos_f.at[c], pos_f.at[c], sibling)

    own_block = z * NY + y

    def eligible(block):
        return elig_ref[lax.div(block, NY) * NY + y, z * NY + lax.rem(block, NY)] > 0

    if not dense:

        def walk_back(i, following):
            block = NZ * NY - 1 - i
            next_ref[block] = following
            live = jnp.logical_and(eligible(block), block != own_block)
            return jnp.where(live, block, following)

        first = lax.fori_loop(0, NZ * NY, walk_back, own_block)

        def rank(block, seen):
            live = jnp.logical_and(eligible(block), block != own_block)
            slot_ref[block] = jnp.where(block == own_block, 0, jnp.where(live, 1 + seen, slots))
            return seen + jnp.where(live, 1, 0)

        lax.fori_loop(0, NZ * NY, rank, 0)
        list_ref[0] = own_block

        def walk(t, block):
            list_ref[t] = block
            return next_ref[block]

        lax.fori_loop(1, slots, walk, first)

    for task in GATHER_ORDER[early:]:
        gather_step(*task)
    arrive(("pos",), pos_f.at[other])
    for step in (0, 1, -1, 2, -2, 3, -3, 4):
        need(("bs", step), b_at(step, other))

    def flip(zz, carry):
        for core in range(NC):
            bt_all[zz, core] = b_all[zz, core].T
        return carry

    lax.fori_loop(0, NZ, flip, 0)

    eye = lax.broadcasted_iota(jnp.int32, (ROWS, ROWS), 0) == lax.broadcasted_iota(
        jnp.int32, (ROWS, ROWS), 1
    )
    unit = LOG2E / math.sqrt(EMBED)

    for core in range(NC):
        pos_cols[core * ROWS : (core + 1) * ROWS, :] = jnp.broadcast_to(
            as_column(pos_f[core, 0:1, :], eye), (ROWS, ROWS)
        )

    def hits(xx):
        lane = lax.broadcasted_iota(jnp.int32, (NC * ROWS, ROWS), 1) + (xx * NC + c) * ROWS
        return pos_cols[...] == lane.astype(F32)

    if not dense:
        row_stat[slots] = jnp.zeros((8, ROWS), F32)
        row_stat[slots, 0:2, :] = jnp.full((2, ROWS), neg_fill, F32)
        col_stat[slots] = jnp.zeros((8, ROWS), F32)
        col_stat[slots, 0:4, :] = jnp.full((4, ROWS), neg_fill, F32)

    def block_of(t):
        return t if dense else list_ref[t]

    def slot_of(zz, yy):
        return zz * NY + yy if dense else slot_ref[zz * NY + yy]

    def first_pass(t, carry):
        block = block_of(t)
        left = b_all[lax.div(block, NY)].reshape(NC * ROWS, EMBED)
        right = s_all[lax.rem(block, NY)].reshape(NX * ROWS, EMBED)
        tile = (
            lax.dot_general(left, right, (((1,), (1,)), ((), ())), preferred_element_type=F32)
            * unit
        )
        if dense:
            tile = jnp.where(eligible(block), tile, neg_fill)
        score[t] = tile
        row_top = jnp.max(tile, axis=1, keepdims=True)
        row_sum = jnp.sum(jnp.exp2(tile - row_top), axis=1, keepdims=True)
        col_top = jnp.max(tile, axis=0, keepdims=True)
        col_sum = jnp.sum(jnp.exp2(tile - col_top), axis=0, keepdims=True)
        for core in range(NC):
            span = slice(core * ROWS, (core + 1) * ROWS)
            row_stat[t, core : core + 1, :] = as_row(row_top[span], eye)
            row_stat[t, 2 + core : 3 + core, :] = as_row(row_sum[span], eye)
        for xx in range(NX):
            span = slice(xx * ROWS, (xx + 1) * ROWS)
            col_stat[t, xx : xx + 1, :] = col_top[:, span]
            col_stat[t, 4 + xx : 5 + xx, :] = col_sum[:, span]
        return carry

    def first_pair(i, carry):
        first_pass(2 * i, 0)
        first_pass(2 * i + 1, 0)
        return carry

    lax.fori_loop(0, slots // 2, first_pair, 0)
    own_slot = own_block if dense else 0
    matched = jnp.zeros((NC * ROWS, 1), F32)
    for xx in range(NX):
        matched = matched + jnp.sum(
            jnp.where(hits(xx), score[own_slot, :, xx * ROWS : (xx + 1) * ROWS], 0.0),
            axis=1, keepdims=True,
        )

    def merge(tops, sums):
        top = tops[0]
        for item in tops[1:]:
            top = jnp.maximum(top, item)
        total = jnp.zeros_like(top)
        for item, amount in zip(tops, sums):
            total = total + amount * jnp.exp2(item - top)
        return top, total

    for zz in range(NZ):
        stats = [row_stat[slot_of(zz, yy)] for yy in range(NY)]
        top, total = merge([a[0:2] for a in stats], [a[2:4] for a in stats])
        row_x[NC * zz : NC * zz + NC, :] = top + jnp.log2(total)
    for yy in range(NY):
        stats = [col_stat[slot_of(zz, yy)] for zz in range(NZ)]
        top, total = merge([a[0:4] for a in stats], [a[4:8] for a in stats])
        col_x[NX * yy : NX * yy + NX, :] = top + jnp.log2(total)
    row_x[16:24, :] = jnp.broadcast_to(jnp.sum(matched, axis=0, keepdims=True), (8, ROWS))

    for (dz, dc), (dy, dx) in zip(row_steps, col_steps):
        to = dev(mod(z + dz, NZ), y, x, core_of(dc))
        send(("row", dz, dc), row_x, row_in.at[z * NC + c], to)
        to = dev(z, mod(y + dy, NY), mod(x + dx, NX), c)
        send(("col", dy, dx), col_x, col_in.at[y * NX + x], to)
    row_in[z * NC + c] = row_x[...]
    col_in[y * NX + x] = col_x[...]
    for (dz, dc), (dy, dx) in reversed(list(zip(row_steps, col_steps))):
        arrive(("row", dz, dc), row_in.at[mod(z - dz, NZ) * NC + core_of(dc)])
        arrive(("col", dy, dx), col_in.at[mod(y - dy, NY) * NX + mod(x - dx, NX)])

    def log_sum(parts):
        top, total = merge(parts, [1.0] * len(parts))
        return top + jnp.log2(total)

    row_part = log_sum([row_in[i, 0:16, :] for i in range(16)])
    col_part = log_sum([col_in[i] for i in range(16)])
    matched_sum = row_in[0, 16:24, :]
    for i in range(1, 16):
        matched_sum = matched_sum + row_in[i, 16:24, :]
    row_lse[...] = row_part
    col_lse[...] = col_part
    line_terms = jnp.sum(jnp.sum(row_part, axis=1, keepdims=True), axis=0, keepdims=True)
    plane_terms = jnp.sum(jnp.sum(col_part, axis=1, keepdims=True), axis=0, keepdims=True)
    sum_x[0, 0] = jnp.broadcast_to(line_terms, (8, ROWS)) - 2.0 * matched_sum
    sum_x[0, 1] = jnp.broadcast_to(plane_terms, (8, ROWS))

    def loss_send(hop):
        send(("l0", hop), sum_x.at[hop, 0], sum_in.at[hop, 0], col_peers[hop])
        send(("l1", hop), sum_x.at[hop, 1], sum_in.at[hop, 1], row_peers[hop])

    def loss_add(hop):
        arrive(("l0", hop), sum_in.at[hop, 0])
        arrive(("l1", hop), sum_in.at[hop, 1])
        sum_x[hop + 1] = sum_x[hop] + sum_in[hop]

    for zz in range(NZ):
        for core in range(NC):
            place = zz * NC + core
            rl_cols[zz, core * ROWS : (core + 1) * ROWS, :] = jnp.broadcast_to(
                as_column(row_lse[place : place + 1, :], eye) + 1.0, (ROWS, ROWS)
            )

    def second_pass(t, own):
        block = block_of(t)
        zz, yy = lax.div(block, NY), lax.rem(block, NY)
        row_part = rl_cols[zz]
        parts = []
        for xx in range(NX):
            tile = score[t, :, xx * ROWS : (xx + 1) * ROWS]
            col_part = col_lse[pl.ds(yy * NX + xx, 1), :] + 1.0
            mixed = jnp.exp2(tile - row_part) + jnp.exp2(tile - col_part)
            if dense:
                mixed = mixed - jnp.where(block == own_block, jnp.where(hits(xx), 1.0, 0.0), 0.0)
            elif own:
                mixed = mixed - jnp.where(hits(xx), 1.0, 0.0)
            parts.append(mixed.astype(BF16))
        weights = jnp.concatenate(parts, axis=1)
        right = s_all[yy].reshape(NX * ROWS, EMBED)
        term = jnp.dot(weights, right, preferred_element_type=F32)
        for core in range(NC):
            part = term[core * ROWS : (core + 1) * ROWS]
            if dense:
                pbuf[zz, core] = pbuf[zz, core] + part
            else:
                pbuf[t, core] = part
        flipped = jnp.concatenate([bt_all[zz, 0], bt_all[zz, 1]], axis=1)
        term = jnp.dot(flipped, weights, preferred_element_type=F32)
        for xx in range(NX):
            part = term[:, xx * ROWS : (xx + 1) * ROWS]
            if dense:
                qbuf[yy, xx] = qbuf[yy, xx] + part
            else:
                qbuf[t, xx] = part

    def other_blocks(i, carry):
        second_pass(2 * i, False)
        second_pass(2 * i + 1, False)
        return carry

    loss_send(0)
    if dense:
        pbuf[...] = jnp.zeros(pbuf.shape, F32)
        qbuf[...] = jnp.zeros(qbuf.shape, F32)
        lax.fori_loop(0, slots // 2, other_blocks, 0)
    else:
        second_pass(0, True)
        second_pass(1, False)
        lax.fori_loop(1, slots // 2, other_blocks, 0)
        pbuf[slots] = jnp.zeros(pbuf.shape[1:], F32)
        qbuf[slots] = jnp.zeros(qbuf.shape[1:], F32)
    step_rows = 32

    def by_rows(lo, rows, body):
        def at(i, carry):
            body(pl.multiple_of(lo + i * step_rows, step_rows))
            return carry

        lax.fori_loop(0, rows // step_rows, at, 0)

    def p_sum(zz, core, at):
        if dense:
            return pbuf[zz, core, pl.ds(at, step_rows), :]
        total = None
        for yy in range(NY):
            term = pbuf[slot_of(zz, yy), core, pl.ds(at, step_rows), :]
            total = term if total is None else total + term
        return total

    def q_sum(yy, xx, at):
        if dense:
            return qbuf[yy, xx, pl.ds(at, step_rows), :]
        total = None
        for zz in range(NZ):
            term = qbuf[slot_of(zz, yy), xx, pl.ds(at, step_rows), :]
            total = term if total is None else total + term
        return total

    def to_f32(ref, place, at):
        return ref[(*place, pl.ds(at, step_rows))].astype(F32)

    order = (4, 3, -3, 2, -2, 1, -1, 0)

    def sib_send(place):
        def fill(at):
            value = p_sum(mod(z + order[place], NZ), other, at)
            sib_s[place, pl.ds(at, step_rows), :] = value.astype(BF16)

        by_rows(0, ROWS, fill)
        send(("gs", place), sib_s.at[place], sib_r.at[place], sibling)

    def z_value(place, at):
        return p_sum(mod(z + order[place], NZ), c, at) + to_f32(sib_r, (place,), at)

    z_places = ((0, 1, 3, 5), (0, 2, 4, 6))

    def z_send(d, hop, i):
        sign, lo, place = 1 - 2 * d, 32 * i, z_places[d][hop]
        started = hop == 0 or (hop == 1 and (lo < 64) == (d == 1))
        need(("gs", place), sib_r.at[place])
        if not started:
            arrive(("gz", d, hop - 1, i), z_r.at[d, hop - 1, pl.ds(lo, 32)])
        value = z_value(place, lo)
        if not started:
            value = value + to_f32(z_r, (d, hop - 1,), lo)
        z_s[d, hop, pl.ds(lo, 32), :] = value.astype(BF16)
        part = pl.ds(lo, 32)
        send(("gz", d, hop, i), z_s.at[d, hop, part], z_r.at[d, hop, part], zdev(sign))

    grads = (("y", ydev, xdev, 0, x), ("x", xdev, ydev, 256, y))
    offsets = (2, 1, -1, 0)
    groups = ((0,), (1, 2), (3,))

    def q_at(axis, step, lane, at):
        if axis == "y":
            return q_sum(mod(y + step, NY), lane, at)
        return q_sum(lane, mod(x + step, NX), at)

    def f_send(kind, h, d, g):
        axis, dev1, dev2, base, place = grads[h]
        sign = 1 - 2 * d
        group = groups[g]
        part = pl.ds(group[0], len(group))
        half = 1 - d if kind == "fa" else d
        if kind == "fb":
            arrive(("f0", h, d, g), f0_r.at[h, d, part])
        for k in group:
            def fill(at):
                step = 2 if kind == "f0" else sign
                value = q_at(axis, step, mod(place + offsets[k], 4), base + half * 128 + at)
                if kind == "f0":
                    f0_s[h, d, k, pl.ds(at, step_rows), :] = value.astype(BF16)
                    return
                if kind == "fb":
                    value = value + to_f32(f0_r, (h, d, k,), at)
                f1_s[h, d, half, k, pl.ds(at, step_rows), :] = value.astype(BF16)

            by_rows(0, 128, fill)
        if kind == "f0":
            send((kind, h, d, g), f0_s.at[h, d, part], f0_r.at[h, d, part], dev1(sign))
        else:
            send((kind, h, d, g), f1_s.at[h, d, half, part], f1_r.at[h, d, half, part], dev1(sign))

    def mid_sum(h, g):
        axis, dev1, dev2, base, place = grads[h]
        group = groups[g]
        part = pl.ds(group[0], len(group))
        for d in range(2):
            arrive(("fa", h, d, g), f1_r.at[h, d, 1 - d, part])
            arrive(("fb", h, d, g), f1_r.at[h, d, d, part])
        for k in group:
            for half in range(2):
                def fill(at):
                    value = q_at(axis, 0, mod(place + offsets[k], 4), base + half * 128 + at)
                    value = value + to_f32(f1_r, (h, 0, half, k,), at)
                    value = value + to_f32(f1_r, (h, 1, half, k,), at)
                    mid[h, k, pl.ds(half * 128 + at, step_rows), :] = value

                by_rows(0, 128, fill)

    def g_send(kind, h, d):
        axis, dev1, dev2, base, place = grads[h]
        sign = 1 - 2 * d
        far_lo, near_lo = d * 128, 128 - d * 128
        if kind == "g0":
            g0_s[h, d] = mid[h, 0, far_lo : far_lo + 128, :].astype(BF16)
            send(("g0", h, d), g0_s.at[h, d], g0_r.at[h, d], dev2(sign))
            return
        arrive(("g0", h, d), g0_r.at[h, d])
        g1_s[h, d, near_lo : near_lo + 128, :] = mid[h, 1 + d, near_lo : near_lo + 128, :].astype(BF16)
        g1_s[h, d, far_lo : far_lo + 128, :] = (
            mid[h, 1 + d, far_lo : far_lo + 128, :] + g0_r[h, d].astype(F32)
        ).astype(BF16)
        send(("g1", h, d), g1_s.at[h, d], g1_r.at[h, d], dev2(sign))

    def g_end(h):
        for d in range(2):
            arrive(("g1", h, d), g1_r.at[h, d])
        seller_t[h * 256 : (h + 1) * 256, :] = (
            mid[h, 3] + g1_r[h, 0].astype(F32) + g1_r[h, 1].astype(F32)
        )

    def z_end():
        need(("gs", 7), sib_r.at[7])
        for d in range(2):
            for i in range(4):
                arrive(("gz", d, 3, i), z_r.at[d, 3, pl.ds(32 * i, 32)])

        def finish(at):
            bgrad_ref[pl.ds(at, step_rows), :] = (
                z_value(7, at) + to_f32(z_r, (0, 3,), at) + to_f32(z_r, (1, 3,), at)
            )

        by_rows(0, ROWS, finish)

    def loss_step(hop):
        loss_add(hop)
        if hop < 3:
            loss_send(hop + 1)

    actions = {
        "sib": sib_send, "z": z_send, "zend": z_end, "mid": mid_sum, "gend": g_end, "loss": loss_step,
    }
    for task in RETURN_ORDER:
        if task[0] in actions:
            actions[task[0]](*task[1:])
        elif task[0] in ("g0", "g1"):
            g_send(*task)
        else:
            f_send(*task)
    sgrad_ref[...] = seller_t[...].T
    loss_ref[...] = (sum_x[4, 0, 0:1, :] + sum_x[4, 1, 0:1, :]) * (
        math.log(2.0) / (2.0 * ROWS * NZ * NY * NX * NC)
    )
    for copy in pending:
        copy.wait_send()


def vmem(shape, dtype):
    return pltpu.VMEM(shape, dtype)


def fused(dense, slots, buyers, sellers, eligibility, positives):
    extra = 0 if dense else 1
    scratch = [
        vmem((NZ, NC, ROWS, EMBED), BF16),
        vmem((NY, NX, ROWS, EMBED), BF16),
        vmem((NZ, NC, EMBED, ROWS), BF16),
        vmem((slots, NC * ROWS, NX * ROWS), F32),
        vmem((NZ if dense else slots + 1, NC, ROWS, EMBED), F32),
        vmem((NY if dense else slots + 1, NX, EMBED, ROWS), F32),
        vmem((NC, 8, ROWS), F32),
        vmem((NC * ROWS, ROWS), F32),
        vmem((slots + extra, 8, ROWS), F32),
        vmem((slots + extra, 8, ROWS), F32),
        vmem((24, ROWS), F32),
        vmem((16, 24, ROWS), F32),
        vmem((16, ROWS), F32),
        vmem((16, 16, ROWS), F32),
        vmem((16, ROWS), F32),
        vmem((16, ROWS), F32),
        vmem((5, 2, 8, ROWS), F32),
        vmem((4, 2, 8, ROWS), F32),
        vmem((NZ, NC * ROWS, ROWS), F32),
        vmem((NZ, ROWS, EMBED), BF16),
        vmem((NZ, ROWS, EMBED), BF16),
        vmem((2, 4, ROWS, EMBED), BF16),
        vmem((2, 4, ROWS, EMBED), BF16),
        vmem((2, 2, 4, 128, ROWS), BF16),
        vmem((2, 2, 4, 128, ROWS), BF16),
        vmem((2, 2, 2, 4, 128, ROWS), BF16),
        vmem((2, 2, 2, 4, 128, ROWS), BF16),
        vmem((2, 4, 256, ROWS), F32),
        vmem((2, 2, 128, ROWS), BF16),
        vmem((2, 2, 128, ROWS), BF16),
        vmem((2, 2, 256, ROWS), BF16),
        vmem((2, 2, 256, ROWS), BF16),
        vmem((EMBED, ROWS), F32),
        pltpu.SMEM((NZ * NY,), jnp.int32),
        pltpu.SMEM((NZ * NY,), jnp.int32),
        pltpu.SMEM((slots,), jnp.int32),
        pltpu.SemaphoreType.DMA((224,)),
        pltpu.SemaphoreType.DMA((224,)),
    ]
    in_vmem = pl.BlockSpec(memory_space=pltpu.VMEM)
    buyer_grad, seller_grad, loss = pl.pallas_call(
        functools.partial(kernel, dense),
        out_shape=(
            jax.ShapeDtypeStruct((ROWS, EMBED), F32),
            jax.ShapeDtypeStruct((ROWS, EMBED), F32),
            jax.ShapeDtypeStruct((1, ROWS), F32),
        ),
        in_specs=[in_vmem, in_vmem, pl.BlockSpec(memory_space=pltpu.SMEM), in_vmem],
        out_specs=(in_vmem, in_vmem, in_vmem),
        scratch_shapes=scratch,
        compiler_params=pltpu.CompilerParams(
            collective_id=1 if dense else 0, has_side_effects=True, vmem_limit_bytes=60 * 1024 * 1024
        ),
        name="two_tower_dense" if dense else "two_tower",
    )(buyers, sellers, eligibility, positives.reshape(1, ROWS))
    return (buyer_grad, seller_grad, loss[0, 0])


def ring_step(value, axis):
    count = lax.axis_size(axis)
    return lax.ppermute(value, axis, [(i, (i + 1) % count) for i in range(count)])


def ring_gather(value, axis):
    count, me = lax.axis_size(axis), lax.axis_index(axis)
    start = jnp.zeros((count, *value.shape), value.dtype)
    start = lax.dynamic_update_index_in_dim(start, value, me, 0)

    def step(k, state):
        block, whole = state
        block = ring_step(block, axis)
        place = lax.rem(me - k + count, count)
        return (block, lax.dynamic_update_index_in_dim(whole, block, place, 0))

    return lax.fori_loop(1, count, step, (value, start))[1]


def ring_scatter(whole, axis):
    count, me = lax.axis_size(axis), lax.axis_index(axis)
    parts = whole.reshape(count, -1, whole.shape[-1])

    def take(place):
        return lax.dynamic_index_in_dim(parts, lax.rem(place + 2 * count, count), 0, False)

    def step(k, total):
        return ring_step(total, axis) + take(me - 1 - k)

    return lax.fori_loop(1, count, step, take(me - 1))


def merged(part, axis, combine):
    gathered = jax.tree.map(lambda a: ring_gather(a, axis), part)

    def take(source):
        return jax.tree.map(lambda a: lax.dynamic_index_in_dim(a, source, 0, False), gathered)

    return lax.fori_loop(
        1, lax.axis_size(axis), lambda source, state: combine(state, take(source)), take(0)
    )


def tile_scores(left, right, factor):
    return (
        lax.dot_general(left, right, (((1,), (1,)), ((), ())), preferred_element_type=jnp.float32)
        * factor
    )


def row_combine(first_part, second_part):
    top = jnp.maximum(first_part[0], second_part[0])
    total = first_part[1] * jnp.exp(first_part[0] - top) + second_part[1] * jnp.exp(
        second_part[0] - top
    )
    return (top, total, first_part[2] + second_part[2])


def col_combine(first_part, second_part):
    top = jnp.maximum(first_part[0], second_part[0])
    total = first_part[1] * jnp.exp(first_part[0] - top) + second_part[1] * jnp.exp(
        second_part[0] - top
    )
    return (top, total)


def coefficient(scores, row_lse, col_lse, is_hit):
    mixed = 0.5 * (jnp.exp(scores - row_lse) + jnp.exp(scores - col_lse)) - jnp.where(
        is_hit, 1.0, 0.0
    )
    return mixed.astype(jnp.bfloat16)


def sweep_groups(stats_step, totals, flags, group_count):

    def outer(state, block_idx):
        outputs = []
        for offset in range(4):
            target = block_idx * 4 + offset
            state, result = stats_step(state, target, flags[target] > 0)
            outputs.append(result)
        stacked = jax.tree.map(lambda *items: jnp.stack(items), *outputs)
        return (state, stacked)

    return lax.scan(outer, totals, jnp.arange(group_count // 4))


def general(buyers, sellers, eligibility, positives):
    row_count, embed_width = buyers.shape
    sub_count = lax.axis_size("sub")
    group_count = lax.axis_size("market")
    group_rows = row_count * sub_count
    market_pos = lax.axis_index("market")
    sub_pos = lax.axis_index("sub")
    factor = 1.0 / math.sqrt(embed_width)
    local_cols = jnp.arange(row_count, dtype=jnp.int32)
    buyer_half = buyers.astype(jnp.bfloat16)
    seller_half = sellers.astype(jnp.bfloat16)
    group_buyers, group_pos = (
        ring_gather(buyer_half, "sub").reshape(-1, embed_width),
        ring_gather(positives, "sub").reshape(-1),
    )
    seller_panel = ring_gather(seller_half, "market").reshape(-1, embed_width)
    own_row = lax.dynamic_index_in_dim(eligibility, market_pos, 0, keepdims=False)

    def panel_block(target):
        return lax.dynamic_slice_in_dim(seller_panel, target * row_count, row_count, 0)

    def stats_step(state, target, is_live):
        row_max, row_sum = state

        def stats_live_branch(unused):
            scores = tile_scores(group_buyers, panel_block(target), factor)
            new_max = jnp.maximum(row_max, jnp.max(scores, axis=1))
            new_sum = row_sum * jnp.exp(row_max - new_max) + jnp.sum(
                jnp.exp(scores - new_max[:, None]), axis=1
            )
            col_top = jnp.max(scores, axis=0)
            col_total = jnp.sum(jnp.exp(scores - col_top[None, :]), axis=0)
            return ((new_max, new_sum), (col_top, col_total))

        def stats_dead_branch(unused):
            return (
                (row_max, row_sum),
                (
                    jnp.full((row_count,), neg_fill, jnp.float32),
                    jnp.zeros((row_count,), jnp.float32),
                ),
            )

        return lax.cond(is_live, stats_live_branch, stats_dead_branch, None)

    start_state = (
        jnp.full((group_rows,), neg_fill, jnp.float32),
        jnp.zeros((group_rows,), jnp.float32),
    )
    (row_max, row_sum), (col_top, col_total) = sweep_groups(
        stats_step, start_state, own_row, group_count
    )
    col_top = col_top.reshape(group_count * row_count)
    col_total = col_total.reshape(group_count * row_count)
    own_scores = tile_scores(group_buyers, seller_half, factor)
    own_ids = (market_pos * sub_count + sub_pos) * row_count + local_cols
    pos_part = jnp.sum(jnp.where(group_pos[:, None] == own_ids[None, :], own_scores, 0.0), axis=1)
    row_max, row_sum, pos_logits = merged((row_max, row_sum, pos_part), "sub", row_combine)
    col_top, col_total = merged((col_top, col_total), "market", col_combine)
    row_lse = row_max + jnp.log(row_sum)
    col_lse = col_top + jnp.log(col_total)
    row_own = lax.dynamic_slice_in_dim(row_lse, sub_pos * row_count, row_count, 0)
    col_own = lax.dynamic_slice_in_dim(col_lse, market_pos * row_count, row_count, 0)
    pos_own = lax.dynamic_slice_in_dim(pos_logits, sub_pos * row_count, row_count, 0)
    local_loss = jnp.sum(row_own) + jnp.sum(col_own) - 2.0 * jnp.sum(pos_own)
    total_loss = jnp.sum(ring_gather(local_loss.reshape(1), "sub"))
    total_loss = jnp.sum(ring_gather(total_loss.reshape(1), "market"))
    loss = total_loss / (2.0 * group_rows * group_count)

    def grad_step(state, target, is_live):

        def grad_live_branch(acc):
            block = panel_block(target)
            scores = tile_scores(group_buyers, block, factor)
            block_lse = lax.dynamic_slice_in_dim(col_lse, target * row_count, row_count, 0)
            block_ids = (target * sub_count + sub_pos) * row_count + local_cols
            weights_half = coefficient(
                scores,
                row_lse[:, None],
                block_lse[None, :],
                group_pos[:, None] == block_ids[None, :],
            )
            return acc + jnp.dot(weights_half, block, preferred_element_type=jnp.float32)

        return (lax.cond(is_live, grad_live_branch, lambda acc: acc, state), None)

    acc, unused = sweep_groups(
        grad_step,
        jnp.zeros((lax.axis_size("sub") * row_count, embed_width), jnp.float32),
        own_row,
        group_count,
    )
    buyer_grad = ring_scatter(acc, "sub")
    row_span = lax.axis_size("market") * row_count

    def one_group(offset):

        def one_live_branch(unused):
            block = panel_block(offset)
            scores = tile_scores(group_buyers, block, factor)
            block_lse = lax.dynamic_slice_in_dim(col_lse, offset * row_count, row_count, 0)
            block_ids = (offset * sub_count + sub_pos) * row_count + local_cols
            weights_half = coefficient(
                scores,
                row_lse[:, None],
                block_lse[None, :],
                group_pos[:, None] == block_ids[None, :],
            )
            return lax.dot_general(
                weights_half,
                group_buyers,
                (((0,), (0,)), ((), ())),
                preferred_element_type=jnp.float32,
            )

        def one_dead_branch(unused):
            return jnp.zeros((row_count, embed_width), jnp.float32)

        return lax.cond(own_row[offset] > 0, one_live_branch, one_dead_branch, None)

    pieces = lax.map(one_group, jnp.arange(row_span // row_count))
    seller_grad = ring_scatter(pieces.reshape(row_span, embed_width), "market")
    return (buyer_grad, seller_grad, loss)


def shards(buyers, sellers, eligibility, positives):
    blocks = (eligibility > 0).astype(jnp.int32).reshape(NZ, NY, NZ, NY)
    busiest = jnp.max(jnp.sum(blocks, axis=(0, 3)))
    return lax.cond(
        busiest <= SLOTS,
        functools.partial(fused, False, SLOTS),
        general,
        buyers, sellers, eligibility, positives,
    )


def solution(mesh):
    return jax.shard_map(
        shards,
        mesh=mesh,
        in_specs=(
            P(("market", "sub"), None),
            P(("market", "sub"), None),
            P(),
            P(("market", "sub")),
        ),
        out_specs=(P(("market", "sub"), None), P(("market", "sub"), None), P()),
        check_vma=False,
    )
```

```python
import functools
import math

import jax
import jax.numpy as jnp
from jax import lax
from jax.experimental import pallas as pl
from jax.experimental.pallas import tpu as pltpu
from jax.sharding import PartitionSpec as P

neg_fill = -1e30
MESH = pl.DeviceIdType.MESH
NZ, NY, NX, NC = 8, 4, 4, 2
ROWS = 128
EMBED = 512
LOG2E = 1.0 / math.log(2.0)
SLOTS = 14
F32 = jnp.float32
BF16 = jnp.bfloat16


GATHER_ORDER = (
    ("b", 0, -1, 0), ("s0", 0, -1), ("bs", 0), ("b", 0, 1, 0), ("s0", 0, 1), ("s0", 1, 1), ("s2", 1, 0, 1),
    ("s0", 1, -1), ("b", 0, -1, 2), ("b", 0, 1, 1), ("b", 0, -1, 1), ("b", 0, 1, 2), ("flip", 0, 1),
    ("s2", 0, 0, -1), ("s2", 0, 0, 1), ("s2", 1, 0, -1), ("b", 1, -1, 0), ("s2", 0, 1, 1), ("b", 1, 1, 0),
    ("s2", 1, -1, 1), ("s2", 0, 1, -1), ("s1", 0, -1), ("s1", 1, -1), ("b", 1, -1, 1), ("b", 1, 1, 1),
    ("b", 1, -1, 2), ("s1", 1, 1), ("s1", 0, 1), ("b", 1, 1, 2), ("s3", 0, 0, -1), ("s2", 1, 1, -1),
    ("s2", 1, 1, 1), ("s2", 1, -1, -1), ("s2", 0, -1, 1), ("s3", 0, 1, 1), ("b", 2, -1, 0), ("b", 2, 1, 1),
    ("s2", 0, -1, -1), ("flip", 0, 0), ("flip", -1, 0), ("b", 2, -1, 1), ("b", 2, 1, 0), ("s2", 1, 2, 1),
    ("b", 2, -1, 2), ("s2", 1, 2, -1), ("b", 2, 1, 2), ("s2", 0, 2, -1), ("s4", 0, 0, -1), ("bs", 2),
    ("s2", 0, 2, 1), ("bs", 1), ("bs", -2), ("s3", 1, 0, 1), ("s3", 1, -1, 1), ("s4", 0, 1, 1),
    ("b", 3, 1, 1), ("b", 3, -1, 0), ("s3", 1, 1, -1), ("flip", -2, 0), ("b", 3, 1, 0), ("b", 3, -1, 1),
    ("s3", 0, -1, 1), ("s3", 1, -1, -1), ("s3", 0, 1, -1), ("s3", 1, 0, -1), ("s3", 1, 1, 1), ("bs", -1),
    ("flip", 2, 0), ("s3", 0, 0, 1), ("s3", 1, 2, 1), ("s3", 0, -1, -1), ("flip", -2, 1), ("flip", 2, 1),
    ("flip", 1, 1), ("bs", 3), ("s3", 1, 2, -1), ("s3", 0, 2, -1), ("s3", 0, 2, 1), ("flip", -3, 0),
    ("bs", -3), ("bs", 4), ("flip", 3, 0), ("s4", 1, 0, 1), ("flip", 4, 0), ("flip", 3, 1), ("s4", 1, 1, -1),
    ("flip", -1, 1), ("s4", 0, -1, 1), ("flip", 1, 0), ("s4", 1, 0, -1), ("s4", 0, -1, -1), ("s4", 1, -1, -1),
    ("s4", 1, -1, 1), ("flip", -3, 1), ("s4", 1, 1, 1), ("s4", 0, 2, 1), ("s4", 0, 1, -1), ("s4", 0, 0, 1),
    ("s4", 0, 2, -1), ("s4", 1, 2, 1), ("s4", 1, 2, -1), ("flip", 4, 1),
)
RETURN_ORDER = (
    ("f0", 1, 1, 0), ("sib", 0), ("f0", 1, 0, 0), ("f0", 0, 0, 0), ("f0", 0, 1, 2), ("sib", 4),
    ("f0", 1, 1, 2), ("f0", 1, 0, 1), ("f0", 0, 1, 0), ("fa", 1, 0, 2), ("sib", 2), ("f0", 0, 0, 1),
    ("f0", 1, 0, 2), ("loss", 0), ("f0", 1, 1, 1), ("fa", 0, 1, 0), ("sib", 1), ("z", 0, 0, 0),
    ("z", 1, 0, 3), ("sib", 7), ("z", 0, 0, 1), ("fa", 1, 1, 0), ("f0", 0, 0, 2), ("f0", 0, 1, 1),
    ("z", 1, 0, 2), ("sib", 5), ("z", 0, 1, 3), ("sib", 3), ("fb", 0, 0, 0), ("z", 1, 1, 0), ("fa", 0, 0, 0),
    ("fb", 1, 1, 0), ("fb", 1, 0, 0), ("fa", 1, 1, 1), ("loss", 1), ("fa", 0, 1, 1), ("z", 0, 1, 2),
    ("z", 1, 1, 1), ("fb", 0, 1, 0), ("fa", 1, 0, 0), ("z", 1, 1, 3), ("z", 0, 1, 0), ("fa", 1, 1, 2),
    ("fa", 0, 0, 1), ("fa", 1, 0, 1), ("z", 0, 1, 1), ("fb", 0, 0, 1), ("z", 1, 1, 2), ("z", 0, 2, 3),
    ("fb", 0, 1, 1), ("z", 1, 2, 0), ("sib", 6), ("fb", 1, 1, 1), ("fb", 1, 0, 1), ("z", 1, 2, 1),
    ("z", 0, 2, 2), ("mid", 1, 0), ("loss", 2), ("z", 0, 2, 0), ("g0", 1, 1), ("g0", 1, 0), ("z", 1, 2, 3),
    ("mid", 0, 0), ("g0", 0, 1), ("z", 1, 2, 2), ("g0", 0, 0), ("z", 0, 2, 1), ("fb", 0, 1, 2),
    ("fb", 0, 0, 2), ("fb", 1, 1, 2), ("fb", 1, 0, 2), ("fa", 0, 1, 2), ("fa", 0, 0, 2), ("z", 1, 3, 0),
    ("z", 0, 3, 3), ("z", 1, 3, 1), ("z", 0, 3, 2), ("mid", 1, 1), ("g1", 1, 1), ("g1", 1, 0), ("z", 0, 3, 0),
    ("z", 1, 3, 3), ("mid", 0, 1), ("loss", 3), ("g1", 0, 0), ("g1", 0, 1), ("z", 0, 3, 1), ("z", 1, 3, 2),
    ("mid", 0, 2), ("mid", 1, 2), ("gend", 1), ("zend",), ("gend", 0),
)


def mod(value, size):
    return lax.rem(value + size, size)


def as_row(column, eye):
    return jnp.sum(jnp.where(eye, column, 0.0), axis=0, keepdims=True)


def as_column(row, eye):
    return jnp.sum(jnp.where(eye, row, 0.0), axis=1, keepdims=True)


def kernel(
    dense,
    buyers_ref, sellers_ref, elig_ref, pos_ref,
    bgrad_ref, sgrad_ref, loss_ref,
    b_all, s_all, bt_all, score, pbuf, qbuf,
    pos_f, pos_cols, row_stat, col_stat, row_x, row_in, col_x, col_in,
    row_lse, col_lse, sum_x, sum_in, rl_cols,
    sib_s, sib_r, z_s, z_r, f0_s, f0_r, f1_s, f1_r, mid, g0_s, g0_r, g1_s, g1_r, seller_t,
    next_ref, slot_ref, list_ref,
    send_sem, recv_sem,
):
    slots = NZ * NY if dense else score.shape[0]
    market = lax.axis_index("market")
    sub = lax.axis_index("sub")
    z, y = lax.div(market, NY), lax.rem(market, NY)
    x, c = lax.div(sub, NC), lax.rem(sub, NC)
    other = 1 - c

    def dev(zz, yy, xx, cc):
        return (zz * NY + yy, xx * NC + cc)

    def zdev(step):
        return dev(mod(z + step, NZ), y, x, c)

    def ydev(step):
        return dev(z, mod(y + step, NY), x, c)

    def xdev(step):
        return dev(z, y, mod(x + step, NX), c)

    sibling = dev(z, y, x, other)

    row_peers = (
        sibling,
        dev(z + 1 - 2 * lax.rem(z, 2), y, x, c),
        dev(z + 2 - 4 * lax.rem(lax.div(z, 2), 2), y, x, c),
        dev(mod(z + 4, NZ), y, x, c),
    )
    col_peers = (
        dev(z, y, x + 1 - 2 * lax.rem(x, 2), c),
        dev(z, y, mod(x + 2, NX), c),
        dev(z, y + 1 - 2 * lax.rem(y, 2), x, c),
        dev(z, mod(y + 2, NY), x, c),
    )

    barrier = pltpu.get_barrier_semaphore()
    row_steps = [(dz, dc) for dz in (4, 3, 5, 2, 6, 1, 7, 0) for dc in (0, 1) if dz or dc]
    col_steps = [(dy, dx) for dy in (2, 1, 3, 0) for dx in (2, 1, 3, 0) if dy or dx]

    def core_of(dc):
        return other if dc else c

    for (dz, dc), (dy, dx) in zip(row_steps, col_steps):
        for peer in (
            dev(mod(z + dz, NZ), y, x, core_of(dc)),
            dev(z, mod(y + dy, NY), mod(x + dx, NX), c),
        ):
            pl.semaphore_signal(barrier, inc=1, device_id=peer, device_id_type=MESH)
    b_all[z, c] = buyers_ref[...].astype(BF16)
    s_all[y, x] = sellers_ref[...].astype(BF16)
    own_pos = pos_ref[...] - market * (ROWS * NX * NC)
    pos_f[c] = jnp.broadcast_to(own_pos.astype(F32), (8, ROWS))
    pl.semaphore_wait(barrier, 30)

    names = {}
    landed = set()
    pending = []

    def sem_of(name):
        return names.setdefault(name, len(names))

    def send(name, src, dst, device):
        place = sem_of(name)
        copy = pltpu.make_async_remote_copy(
            src_ref=src, dst_ref=dst, send_sem=send_sem.at[place], recv_sem=recv_sem.at[place],
            device_id=device, device_id_type=MESH,
        )
        copy.start()
        pending.append(copy)

    def arrive(name, dst):
        place = sem_of(name)
        pltpu.make_async_remote_copy(
            src_ref=dst, dst_ref=dst, send_sem=send_sem.at[place], recv_sem=recv_sem.at[place],
            device_id=sibling, device_id_type=MESH,
        ).wait_recv()

    def need(name, dst):
        if name not in landed:
            landed.add(name)
            arrive(name, dst)

    def b_at(step, core, lo=0, rows=ROWS):
        return b_all.at[mod(z + step, NZ), core, pl.ds(lo, rows)]

    def s_at(first_axis, first_step, second_step, lo, rows):
        if first_axis == "x":
            return s_all.at[mod(y + second_step, NY), mod(x + first_step, NX), pl.ds(lo, rows)]
        return s_all.at[mod(y + first_step, NY), mod(x + second_step, NX), pl.ds(lo, rows)]

    halves = (("x", xdev, ydev, 0), ("y", ydev, xdev, 64))

    z_parts = {1: ((0, 32), (32, 32), (64, 64)), -1: ((96, 32), (64, 32), (0, 64))}

    def z_ref(hop, sign, i):
        lo, rows = z_parts[sign][i]
        return b_at(-hop * sign, c, lo, rows)

    def have(step):
        if abs(step) == 4:
            wanted = [(4, sign, i) for sign in (1, -1) for i in range(2)]
        else:
            wanted = [(abs(step), -1 if step > 0 else 1, i) for i in range(3)] if step else []
        for hop, sign, i in wanted:
            need(("b", hop, sign, i), z_ref(hop, sign, i))

    def s_ref(kind, h, step1, sign):
        axis, dev1, dev2, lo = halves[h]
        part = lo if sign == 1 else lo + 32
        if kind == "s0":
            return s_at(axis, -sign, 0, lo, 64)
        if kind == "s1":
            return s_at(axis, 2, 0, part, 32)
        if kind == "s2":
            return s_at(axis, step1, -sign, lo, 64)
        return s_at(axis, step1, 2, part, 32)

    def gather_step(kind, *key):
        if kind == "b":
            hop, sign, i = key
            ref = z_ref(hop, sign, i)
            if hop:
                need(("b", hop, sign, i), ref)
            send(("b", hop + 1, sign, i), ref, ref, zdev(sign))
        elif kind == "bs":
            step = key[0]
            have(step)
            send(("bs", step), b_at(step, c), b_at(step, c), sibling)
        elif kind == "flip":
            step, theirs = key
            if theirs:
                need(("bs", step), b_at(step, other))
            else:
                have(step)
            flip(step, other if theirs else c)
        elif kind == "s0" or kind == "s1":
            h, sign = key
            axis, dev1, dev2, lo = halves[h]
            if kind == "s0":
                ref = s_at(axis, 0, 0, lo, 64)
            else:
                need(("s0", h, sign), s_ref("s0", h, 0, sign))
                ref = s_at(axis, -sign, 0, lo if sign == 1 else lo + 32, 32)
            send((kind, h, sign), ref, ref, dev1(sign))
        else:
            h, step1, sign = key
            axis, dev1, dev2, lo = halves[h]
            if kind == "s2":
                if abs(step1) == 1:
                    need(("s0", h, -step1), s_ref("s0", h, 0, -step1))
                elif step1 == 2:
                    for way in (1, -1):
                        need(("s1", h, way), s_ref("s1", h, 0, way))
                ref = s_at(axis, step1, 0, lo, 64)
            elif kind == "s3":
                need(("s2", h, step1, sign), s_ref("s2", h, step1, sign))
                ref = s_at(axis, step1, -sign, lo if sign == 1 else lo + 32, 32)
            else:
                need(("s3", h, step1, sign), s_ref("s3", h, step1, sign))
                return
            send((kind, h, step1, sign), ref, ref, dev2(sign))

    def flip(step, core):
        zz = mod(z + step, NZ)
        bt_all[zz, core] = b_all[zz, core].T

    early = 8
    for task in GATHER_ORDER[:early]:
        gather_step(*task)
    send(("pos",), pos_f.at[c], pos_f.at[c], sibling)

    own_block = z * NY + y

    def eligible(block):
        return elig_ref[lax.div(block, NY) * NY + y, z * NY + lax.rem(block, NY)] > 0

    if not dense:

        def walk_back(i, following):
            block = NZ * NY - 1 - i
            next_ref[block] = following
            live = jnp.logical_and(eligible(block), block != own_block)
            return jnp.where(live, block, following)

        first = lax.fori_loop(0, NZ * NY, walk_back, own_block)

        def rank(block, seen):
            live = jnp.logical_and(eligible(block), block != own_block)
            slot_ref[block] = jnp.where(block == own_block, 0, jnp.where(live, 1 + seen, slots))
            return seen + jnp.where(live, 1, 0)

        lax.fori_loop(0, NZ * NY, rank, 0)
        list_ref[0] = own_block

        def walk(t, block):
            list_ref[t] = block
            return next_ref[block]

        lax.fori_loop(1, slots, walk, first)

    for task in GATHER_ORDER[early:]:
        gather_step(*task)
    arrive(("pos",), pos_f.at[other])

    eye = lax.broadcasted_iota(jnp.int32, (ROWS, ROWS), 0) == lax.broadcasted_iota(
        jnp.int32, (ROWS, ROWS), 1
    )
    unit = LOG2E / math.sqrt(EMBED)

    for core in range(NC):
        pos_cols[core * ROWS : (core + 1) * ROWS, :] = jnp.broadcast_to(
            as_column(pos_f[core, 0:1, :], eye), (ROWS, ROWS)
        )

    def hits(xx):
        lane = lax.broadcasted_iota(jnp.int32, (NC * ROWS, ROWS), 1) + (xx * NC + c) * ROWS
        return pos_cols[...] == lane.astype(F32)

    if not dense:
        row_stat[slots] = jnp.zeros((8, ROWS), F32)
        row_stat[slots, 0:2, :] = jnp.full((2, ROWS), neg_fill, F32)
        col_stat[slots] = jnp.zeros((8, ROWS), F32)
        col_stat[slots, 0:4, :] = jnp.full((4, ROWS), neg_fill, F32)

    def block_of(t):
        return t if dense else list_ref[t]

    def slot_of(zz, yy):
        return zz * NY + yy if dense else slot_ref[zz * NY + yy]

    def first_pass(t, carry):
        block = block_of(t)
        left = b_all[lax.div(block, NY)].reshape(NC * ROWS, EMBED)
        right = s_all[lax.rem(block, NY)].reshape(NX * ROWS, EMBED)
        tile = (
            lax.dot_general(left, right, (((1,), (1,)), ((), ())), preferred_element_type=F32)
            * unit
        )
        if dense:
            tile = jnp.where(eligible(block), tile, neg_fill)
        score[t] = tile
        row_top = jnp.max(tile, axis=1, keepdims=True)
        row_sum = jnp.sum(jnp.exp2(tile - row_top), axis=1, keepdims=True)
        col_top = jnp.max(tile, axis=0, keepdims=True)
        col_sum = jnp.sum(jnp.exp2(tile - col_top), axis=0, keepdims=True)
        for core in range(NC):
            span = slice(core * ROWS, (core + 1) * ROWS)
            row_stat[t, core : core + 1, :] = as_row(row_top[span], eye)
            row_stat[t, 2 + core : 3 + core, :] = as_row(row_sum[span], eye)
        for xx in range(NX):
            span = slice(xx * ROWS, (xx + 1) * ROWS)
            col_stat[t, xx : xx + 1, :] = col_top[:, span]
            col_stat[t, 4 + xx : 5 + xx, :] = col_sum[:, span]
        return carry

    def first_pair(i, carry):
        first_pass(2 * i, 0)
        first_pass(2 * i + 1, 0)
        return carry

    lax.fori_loop(0, slots // 2, first_pair, 0)
    own_slot = own_block if dense else 0
    matched = jnp.zeros((NC * ROWS, 1), F32)
    for xx in range(NX):
        matched = matched + jnp.sum(
            jnp.where(hits(xx), score[own_slot, :, xx * ROWS : (xx + 1) * ROWS], 0.0),
            axis=1, keepdims=True,
        )

    def merge(tops, sums):
        top = tops[0]
        for item in tops[1:]:
            top = jnp.maximum(top, item)
        total = jnp.zeros_like(top)
        for item, amount in zip(tops, sums):
            total = total + amount * jnp.exp2(item - top)
        return top, total

    for zz in range(NZ):
        stats = [row_stat[slot_of(zz, yy)] for yy in range(NY)]
        top, total = merge([a[0:2] for a in stats], [a[2:4] for a in stats])
        row_x[NC * zz : NC * zz + NC, :] = top + jnp.log2(total)
    for yy in range(NY):
        stats = [col_stat[slot_of(zz, yy)] for zz in range(NZ)]
        top, total = merge([a[0:4] for a in stats], [a[4:8] for a in stats])
        col_x[NX * yy : NX * yy + NX, :] = top + jnp.log2(total)
    row_x[16:24, :] = jnp.broadcast_to(jnp.sum(matched, axis=0, keepdims=True), (8, ROWS))

    for (dz, dc), (dy, dx) in zip(row_steps, col_steps):
        to = dev(mod(z + dz, NZ), y, x, core_of(dc))
        send(("row", dz, dc), row_x, row_in.at[z * NC + c], to)
        to = dev(z, mod(y + dy, NY), mod(x + dx, NX), c)
        send(("col", dy, dx), col_x, col_in.at[y * NX + x], to)
    row_in[z * NC + c] = row_x[...]
    col_in[y * NX + x] = col_x[...]
    for (dz, dc), (dy, dx) in reversed(list(zip(row_steps, col_steps))):
        arrive(("row", dz, dc), row_in.at[mod(z - dz, NZ) * NC + core_of(dc)])
        arrive(("col", dy, dx), col_in.at[mod(y - dy, NY) * NX + mod(x - dx, NX)])

    def log_sum(parts):
        top, total = merge(parts, [1.0] * len(parts))
        return top + jnp.log2(total)

    row_part = log_sum([row_in[i, 0:16, :] for i in range(16)])
    col_part = log_sum([col_in[i] for i in range(16)])
    matched_sum = row_in[0, 16:24, :]
    for i in range(1, 16):
        matched_sum = matched_sum + row_in[i, 16:24, :]
    row_lse[...] = row_part
    col_lse[...] = col_part
    line_terms = jnp.sum(jnp.sum(row_part, axis=1, keepdims=True), axis=0, keepdims=True)
    plane_terms = jnp.sum(jnp.sum(col_part, axis=1, keepdims=True), axis=0, keepdims=True)
    sum_x[0, 0] = jnp.broadcast_to(line_terms, (8, ROWS)) - 2.0 * matched_sum
    sum_x[0, 1] = jnp.broadcast_to(plane_terms, (8, ROWS))

    def loss_send(hop):
        send(("l0", hop), sum_x.at[hop, 0], sum_in.at[hop, 0], col_peers[hop])
        send(("l1", hop), sum_x.at[hop, 1], sum_in.at[hop, 1], row_peers[hop])

    def loss_add(hop):
        arrive(("l0", hop), sum_in.at[hop, 0])
        arrive(("l1", hop), sum_in.at[hop, 1])
        sum_x[hop + 1] = sum_x[hop] + sum_in[hop]

    for zz in range(NZ):
        for core in range(NC):
            place = zz * NC + core
            rl_cols[zz, core * ROWS : (core + 1) * ROWS, :] = jnp.broadcast_to(
                as_column(row_lse[place : place + 1, :], eye) + 1.0, (ROWS, ROWS)
            )

    def second_pass(t, own):
        block = block_of(t)
        zz, yy = lax.div(block, NY), lax.rem(block, NY)
        row_part = rl_cols[zz]
        parts = []
        for xx in range(NX):
            tile = score[t, :, xx * ROWS : (xx + 1) * ROWS]
            col_part = col_lse[pl.ds(yy * NX + xx, 1), :] + 1.0
            mixed = jnp.exp2(tile - row_part) + jnp.exp2(tile - col_part)
            if dense:
                mixed = mixed - jnp.where(block == own_block, jnp.where(hits(xx), 1.0, 0.0), 0.0)
            elif own:
                mixed = mixed - jnp.where(hits(xx), 1.0, 0.0)
            parts.append(mixed.astype(BF16))
        weights = jnp.concatenate(parts, axis=1)
        right = s_all[yy].reshape(NX * ROWS, EMBED)
        term = jnp.dot(weights, right, preferred_element_type=F32)
        for core in range(NC):
            part = term[core * ROWS : (core + 1) * ROWS]
            if dense:
                pbuf[zz, core] = pbuf[zz, core] + part
            else:
                pbuf[t, core] = part
        flipped = jnp.concatenate([bt_all[zz, 0], bt_all[zz, 1]], axis=1)
        term = jnp.dot(flipped, weights, preferred_element_type=F32)
        for xx in range(NX):
            part = term[:, xx * ROWS : (xx + 1) * ROWS]
            if dense:
                qbuf[yy, xx] = qbuf[yy, xx] + part
            else:
                qbuf[t, xx] = part

    def other_blocks(i, carry):
        second_pass(2 * i, False)
        second_pass(2 * i + 1, False)
        return carry

    loss_send(0)
    if dense:
        pbuf[...] = jnp.zeros(pbuf.shape, F32)
        qbuf[...] = jnp.zeros(qbuf.shape, F32)
        lax.fori_loop(0, slots // 2, other_blocks, 0)
    else:
        second_pass(0, True)
        second_pass(1, False)
        lax.fori_loop(1, slots // 2, other_blocks, 0)
        pbuf[slots] = jnp.zeros(pbuf.shape[1:], F32)
        qbuf[slots] = jnp.zeros(qbuf.shape[1:], F32)
    step_rows = 32

    def by_rows(lo, rows, body):
        def at(i, carry):
            body(pl.multiple_of(lo + i * step_rows, step_rows))
            return carry

        lax.fori_loop(0, rows // step_rows, at, 0)

    def p_sum(zz, core, at):
        if dense:
            return pbuf[zz, core, pl.ds(at, step_rows), :]
        total = None
        for yy in range(NY):
            term = pbuf[slot_of(zz, yy), core, pl.ds(at, step_rows), :]
            total = term if total is None else total + term
        return total

    def q_sum(yy, xx, at):
        if dense:
            return qbuf[yy, xx, pl.ds(at, step_rows), :]
        total = None
        for zz in range(NZ):
            term = qbuf[slot_of(zz, yy), xx, pl.ds(at, step_rows), :]
            total = term if total is None else total + term
        return total

    def to_f32(ref, place, at):
        return ref[(*place, pl.ds(at, step_rows))].astype(F32)

    order = (4, 3, -3, 2, -2, 1, -1, 0)

    def sib_send(place):
        def fill(at):
            value = p_sum(mod(z + order[place], NZ), other, at)
            sib_s[place, pl.ds(at, step_rows), :] = value.astype(BF16)

        by_rows(0, ROWS, fill)
        send(("gs", place), sib_s.at[place], sib_r.at[place], sibling)

    def z_value(place, at):
        return p_sum(mod(z + order[place], NZ), c, at) + to_f32(sib_r, (place,), at)

    z_places = ((0, 1, 3, 5), (0, 2, 4, 6))

    def z_send(d, hop, i):
        sign, lo, place = 1 - 2 * d, 32 * i, z_places[d][hop]
        started = hop == 0 or (hop == 1 and (lo < 64) == (d == 1))
        need(("gs", place), sib_r.at[place])
        if not started:
            arrive(("gz", d, hop - 1, i), z_r.at[d, hop - 1, pl.ds(lo, 32)])
        value = z_value(place, lo)
        if not started:
            value = value + to_f32(z_r, (d, hop - 1,), lo)
        z_s[d, hop, pl.ds(lo, 32), :] = value.astype(BF16)
        part = pl.ds(lo, 32)
        send(("gz", d, hop, i), z_s.at[d, hop, part], z_r.at[d, hop, part], zdev(sign))

    grads = (("y", ydev, xdev, 0, x), ("x", xdev, ydev, 256, y))
    offsets = (2, 1, -1, 0)
    groups = ((0,), (1, 2), (3,))

    def q_at(axis, step, lane, at):
        if axis == "y":
            return q_sum(mod(y + step, NY), lane, at)
        return q_sum(lane, mod(x + step, NX), at)

    def f_send(kind, h, d, g):
        axis, dev1, dev2, base, place = grads[h]
        sign = 1 - 2 * d
        group = groups[g]
        part = pl.ds(group[0], len(group))
        half = 1 - d if kind == "fa" else d
        if kind == "fb":
            arrive(("f0", h, d, g), f0_r.at[h, d, part])
        for k in group:
            def fill(at):
                step = 2 if kind == "f0" else sign
                value = q_at(axis, step, mod(place + offsets[k], 4), base + half * 128 + at)
                if kind == "f0":
                    f0_s[h, d, k, pl.ds(at, step_rows), :] = value.astype(BF16)
                    return
                if kind == "fb":
                    value = value + to_f32(f0_r, (h, d, k,), at)
                f1_s[h, d, half, k, pl.ds(at, step_rows), :] = value.astype(BF16)

            by_rows(0, 128, fill)
        if kind == "f0":
            send((kind, h, d, g), f0_s.at[h, d, part], f0_r.at[h, d, part], dev1(sign))
        else:
            send((kind, h, d, g), f1_s.at[h, d, half, part], f1_r.at[h, d, half, part], dev1(sign))

    def mid_sum(h, g):
        axis, dev1, dev2, base, place = grads[h]
        group = groups[g]
        part = pl.ds(group[0], len(group))
        for d in range(2):
            arrive(("fa", h, d, g), f1_r.at[h, d, 1 - d, part])
            arrive(("fb", h, d, g), f1_r.at[h, d, d, part])
        for k in group:
            for half in range(2):
                def fill(at):
                    value = q_at(axis, 0, mod(place + offsets[k], 4), base + half * 128 + at)
                    value = value + to_f32(f1_r, (h, 0, half, k,), at)
                    value = value + to_f32(f1_r, (h, 1, half, k,), at)
                    mid[h, k, pl.ds(half * 128 + at, step_rows), :] = value

                by_rows(0, 128, fill)

    def g_send(kind, h, d):
        axis, dev1, dev2, base, place = grads[h]
        sign = 1 - 2 * d
        far_lo, near_lo = d * 128, 128 - d * 128
        if kind == "g0":
            g0_s[h, d] = mid[h, 0, far_lo : far_lo + 128, :].astype(BF16)
            send(("g0", h, d), g0_s.at[h, d], g0_r.at[h, d], dev2(sign))
            return
        arrive(("g0", h, d), g0_r.at[h, d])
        g1_s[h, d, near_lo : near_lo + 128, :] = mid[h, 1 + d, near_lo : near_lo + 128, :].astype(BF16)
        g1_s[h, d, far_lo : far_lo + 128, :] = (
            mid[h, 1 + d, far_lo : far_lo + 128, :] + g0_r[h, d].astype(F32)
        ).astype(BF16)
        send(("g1", h, d), g1_s.at[h, d], g1_r.at[h, d], dev2(sign))

    def g_end(h):
        for d in range(2):
            arrive(("g1", h, d), g1_r.at[h, d])
        seller_t[h * 256 : (h + 1) * 256, :] = (
            mid[h, 3] + g1_r[h, 0].astype(F32) + g1_r[h, 1].astype(F32)
        )

    def z_end():
        need(("gs", 7), sib_r.at[7])
        for d in range(2):
            for i in range(4):
                arrive(("gz", d, 3, i), z_r.at[d, 3, pl.ds(32 * i, 32)])

        def finish(at):
            bgrad_ref[pl.ds(at, step_rows), :] = (
                z_value(7, at) + to_f32(z_r, (0, 3,), at) + to_f32(z_r, (1, 3,), at)
            )

        by_rows(0, ROWS, finish)

    def loss_step(hop):
        loss_add(hop)
        if hop < 3:
            loss_send(hop + 1)

    actions = {
        "sib": sib_send, "z": z_send, "zend": z_end, "mid": mid_sum, "gend": g_end, "loss": loss_step,
    }
    for task in RETURN_ORDER:
        if task[0] in actions:
            actions[task[0]](*task[1:])
        elif task[0] in ("g0", "g1"):
            g_send(*task)
        else:
            f_send(*task)
    sgrad_ref[...] = seller_t[...].T
    loss_ref[...] = (sum_x[4, 0, 0:1, :] + sum_x[4, 1, 0:1, :]) * (
        math.log(2.0) / (2.0 * ROWS * NZ * NY * NX * NC)
    )
    for copy in pending:
        copy.wait_send()


def vmem(shape, dtype):
    return pltpu.VMEM(shape, dtype)


def fused(dense, slots, buyers, sellers, eligibility, positives):
    extra = 0 if dense else 1
    scratch = [
        vmem((NZ, NC, ROWS, EMBED), BF16),
        vmem((NY, NX, ROWS, EMBED), BF16),
        vmem((NZ, NC, EMBED, ROWS), BF16),
        vmem((slots, NC * ROWS, NX * ROWS), F32),
        vmem((NZ if dense else slots + 1, NC, ROWS, EMBED), F32),
        vmem((NY if dense else slots + 1, NX, EMBED, ROWS), F32),
        vmem((NC, 8, ROWS), F32),
        vmem((NC * ROWS, ROWS), F32),
        vmem((slots + extra, 8, ROWS), F32),
        vmem((slots + extra, 8, ROWS), F32),
        vmem((24, ROWS), F32),
        vmem((16, 24, ROWS), F32),
        vmem((16, ROWS), F32),
        vmem((16, 16, ROWS), F32),
        vmem((16, ROWS), F32),
        vmem((16, ROWS), F32),
        vmem((5, 2, 8, ROWS), F32),
        vmem((4, 2, 8, ROWS), F32),
        vmem((NZ, NC * ROWS, ROWS), F32),
        vmem((NZ, ROWS, EMBED), BF16),
        vmem((NZ, ROWS, EMBED), BF16),
        vmem((2, 4, ROWS, EMBED), BF16),
        vmem((2, 4, ROWS, EMBED), BF16),
        vmem((2, 2, 4, 128, ROWS), BF16),
        vmem((2, 2, 4, 128, ROWS), BF16),
        vmem((2, 2, 2, 4, 128, ROWS), BF16),
        vmem((2, 2, 2, 4, 128, ROWS), BF16),
        vmem((2, 4, 256, ROWS), F32),
        vmem((2, 2, 128, ROWS), BF16),
        vmem((2, 2, 128, ROWS), BF16),
        vmem((2, 2, 256, ROWS), BF16),
        vmem((2, 2, 256, ROWS), BF16),
        vmem((EMBED, ROWS), F32),
        pltpu.SMEM((NZ * NY,), jnp.int32),
        pltpu.SMEM((NZ * NY,), jnp.int32),
        pltpu.SMEM((slots,), jnp.int32),
        pltpu.SemaphoreType.DMA((224,)),
        pltpu.SemaphoreType.DMA((224,)),
    ]
    in_vmem = pl.BlockSpec(memory_space=pltpu.VMEM)
    buyer_grad, seller_grad, loss = pl.pallas_call(
        functools.partial(kernel, dense),
        out_shape=(
            jax.ShapeDtypeStruct((ROWS, EMBED), F32),
            jax.ShapeDtypeStruct((ROWS, EMBED), F32),
            jax.ShapeDtypeStruct((1, ROWS), F32),
        ),
        in_specs=[in_vmem, in_vmem, pl.BlockSpec(memory_space=pltpu.SMEM), in_vmem],
        out_specs=(in_vmem, in_vmem, in_vmem),
        scratch_shapes=scratch,
        compiler_params=pltpu.CompilerParams(
            collective_id=1 if dense else 0, has_side_effects=True, vmem_limit_bytes=60 * 1024 * 1024
        ),
        name="two_tower_dense" if dense else "two_tower",
    )(buyers, sellers, eligibility, positives.reshape(1, ROWS))
    return (buyer_grad, seller_grad, loss[0, 0])


def shards(buyers, sellers, eligibility, positives):
    blocks = (eligibility > 0).astype(jnp.int32).reshape(NZ, NY, NZ, NY)
    busiest = jnp.max(jnp.sum(blocks, axis=(0, 3)))
    return lax.cond(
        busiest <= SLOTS,
        functools.partial(fused, False, SLOTS),
        functools.partial(fused, True, NZ * NY),
        buyers, sellers, eligibility, positives,
    )


def solution(mesh):
    return jax.shard_map(
        shards,
        mesh=mesh,
        in_specs=(
            P(("market", "sub"), None),
            P(("market", "sub"), None),
            P(),
            P(("market", "sub")),
        ),
        out_specs=(P(("market", "sub"), None), P(("market", "sub"), None), P()),
        check_vma=False,
    )
```

```python
import functools
import math

import jax
import jax.numpy as jnp
from jax import lax
from jax.experimental import pallas as pl
from jax.experimental.pallas import tpu as pltpu
from jax.sharding import PartitionSpec as P

neg_fill = -1e30
MESH = pl.DeviceIdType.MESH
NZ, NY, NX, NC = 8, 4, 4, 2
ROWS = 128
EMBED = 512
LOG2E = 1.0 / math.log(2.0)
SLOTS = 14
F32 = jnp.float32
BF16 = jnp.bfloat16


GATHER_ORDER = (
    ("b", 0, -1, 0), ("s0", 0, -1), ("bs", 0), ("b", 0, 1, 0), ("s0", 0, 1), ("s0", 1, 1), ("s2", 1, 0, 1),
    ("s0", 1, -1), ("b", 0, -1, 2), ("b", 0, 1, 1), ("b", 0, -1, 1), ("b", 0, 1, 2), ("flip", 0, 1),
    ("s2", 0, 0, -1), ("s2", 0, 0, 1), ("s2", 1, 0, -1), ("b", 1, -1, 0), ("s2", 0, 1, 1), ("b", 1, 1, 0),
    ("s2", 1, -1, 1), ("s2", 0, 1, -1), ("s1", 0, -1), ("s1", 1, -1), ("b", 1, -1, 1), ("b", 1, 1, 1),
    ("b", 1, -1, 2), ("s1", 1, 1), ("s1", 0, 1), ("b", 1, 1, 2), ("s3", 0, 0, -1), ("s2", 1, 1, -1),
    ("s2", 1, 1, 1), ("s2", 1, -1, -1), ("s2", 0, -1, 1), ("s3", 0, 1, 1), ("b", 2, -1, 0), ("b", 2, 1, 1),
    ("s2", 0, -1, -1), ("flip", 0, 0), ("flip", -1, 0), ("b", 2, -1, 1), ("b", 2, 1, 0), ("s2", 1, 2, 1),
    ("b", 2, -1, 2), ("s2", 1, 2, -1), ("b", 2, 1, 2), ("s2", 0, 2, -1), ("s4", 0, 0, -1), ("bs", 2),
    ("s2", 0, 2, 1), ("bs", 1), ("bs", -2), ("s3", 1, 0, 1), ("s3", 1, -1, 1), ("s4", 0, 1, 1),
    ("b", 3, 1, 1), ("b", 3, -1, 0), ("s3", 1, 1, -1), ("flip", -2, 0), ("b", 3, 1, 0), ("b", 3, -1, 1),
    ("s3", 0, -1, 1), ("s3", 1, -1, -1), ("s3", 0, 1, -1), ("s3", 1, 0, -1), ("s3", 1, 1, 1), ("bs", -1),
    ("flip", 2, 0), ("s3", 0, 0, 1), ("s3", 1, 2, 1), ("s3", 0, -1, -1), ("flip", -2, 1), ("flip", 2, 1),
    ("flip", 1, 1), ("bs", 3), ("s3", 1, 2, -1), ("s3", 0, 2, -1), ("s3", 0, 2, 1), ("flip", -3, 0),
    ("bs", -3), ("bs", 4), ("flip", 3, 0), ("s4", 1, 0, 1), ("flip", 4, 0), ("flip", 3, 1), ("s4", 1, 1, -1),
    ("flip", -1, 1), ("s4", 0, -1, 1), ("flip", 1, 0), ("s4", 1, 0, -1), ("s4", 0, -1, -1), ("s4", 1, -1, -1),
    ("s4", 1, -1, 1), ("flip", -3, 1), ("s4", 1, 1, 1), ("s4", 0, 2, 1), ("s4", 0, 1, -1), ("s4", 0, 0, 1),
    ("s4", 0, 2, -1), ("s4", 1, 2, 1), ("s4", 1, 2, -1), ("flip", 4, 1),
)
RETURN_ORDER = (
    ("f0", 1, 1, 0), ("sib", 0), ("f0", 1, 0, 0), ("f0", 0, 0, 0), ("f0", 0, 1, 2), ("sib", 4),
    ("f0", 1, 1, 2), ("f0", 1, 0, 1), ("f0", 0, 1, 0), ("fa", 1, 0, 2), ("sib", 2), ("f0", 0, 0, 1),
    ("f0", 1, 0, 2), ("loss", 0), ("f0", 1, 1, 1), ("fa", 0, 1, 0), ("sib", 1), ("z", 0, 0, 0),
    ("z", 1, 0, 3), ("sib", 7), ("z", 0, 0, 1), ("fa", 1, 1, 0), ("f0", 0, 0, 2), ("f0", 0, 1, 1),
    ("z", 1, 0, 2), ("sib", 5), ("z", 0, 1, 3), ("sib", 3), ("fb", 0, 0, 0), ("z", 1, 1, 0), ("fa", 0, 0, 0),
    ("fb", 1, 1, 0), ("fb", 1, 0, 0), ("fa", 1, 1, 1), ("loss", 1), ("fa", 0, 1, 1), ("z", 0, 1, 2),
    ("z", 1, 1, 1), ("fb", 0, 1, 0), ("fa", 1, 0, 0), ("z", 1, 1, 3), ("z", 0, 1, 0), ("fa", 1, 1, 2),
    ("fa", 0, 0, 1), ("fa", 1, 0, 1), ("z", 0, 1, 1), ("fb", 0, 0, 1), ("z", 1, 1, 2), ("z", 0, 2, 3),
    ("fb", 0, 1, 1), ("z", 1, 2, 0), ("sib", 6), ("fb", 1, 1, 1), ("fb", 1, 0, 1), ("z", 1, 2, 1),
    ("z", 0, 2, 2), ("mid", 1, 0), ("loss", 2), ("z", 0, 2, 0), ("g0", 1, 1), ("g0", 1, 0), ("z", 1, 2, 3),
    ("mid", 0, 0), ("g0", 0, 1), ("z", 1, 2, 2), ("g0", 0, 0), ("z", 0, 2, 1), ("fb", 0, 1, 2),
    ("fb", 0, 0, 2), ("fb", 1, 1, 2), ("fb", 1, 0, 2), ("fa", 0, 1, 2), ("fa", 0, 0, 2), ("z", 1, 3, 0),
    ("z", 0, 3, 3), ("z", 1, 3, 1), ("z", 0, 3, 2), ("mid", 1, 1), ("g1", 1, 1), ("g1", 1, 0), ("z", 0, 3, 0),
    ("z", 1, 3, 3), ("mid", 0, 1), ("loss", 3), ("g1", 0, 0), ("g1", 0, 1), ("z", 0, 3, 1), ("z", 1, 3, 2),
    ("mid", 0, 2), ("mid", 1, 2), ("gend", 1), ("zend",), ("gend", 0),
)


def mod(value, size):
    return lax.rem(value + size, size)


def as_row(column, eye):
    return jnp.sum(jnp.where(eye, column, 0.0), axis=0, keepdims=True)


def as_column(row, eye):
    return jnp.sum(jnp.where(eye, row, 0.0), axis=1, keepdims=True)


def kernel(
    dense,
    buyers_ref, sellers_ref, elig_ref, pos_ref,
    bgrad_ref, sgrad_ref, loss_ref,
    b_all, s_all, bt_all, score, pbuf, qbuf,
    pos_f, pos_cols, row_stat, col_stat, row_x, row_in, col_x, col_in,
    row_lse, col_lse, sum_x, sum_in, rl_cols,
    sib_s, sib_r, z_s, z_r, f0_s, f0_r, f1_s, f1_r, mid, g0_s, g0_r, g1_s, g1_r, seller_t,
    next_ref, slot_ref, list_ref,
    send_sem, recv_sem,
):
    slots = NZ * NY if dense else score.shape[0]
    market = lax.axis_index("market")
    sub = lax.axis_index("sub")
    z, y = lax.div(market, NY), lax.rem(market, NY)
    x, c = lax.div(sub, NC), lax.rem(sub, NC)
    other = 1 - c

    def dev(zz, yy, xx, cc):
        return (zz * NY + yy, xx * NC + cc)

    def zdev(step):
        return dev(mod(z + step, NZ), y, x, c)

    def ydev(step):
        return dev(z, mod(y + step, NY), x, c)

    def xdev(step):
        return dev(z, y, mod(x + step, NX), c)

    sibling = dev(z, y, x, other)

    row_peers = (
        sibling,
        dev(z + 1 - 2 * lax.rem(z, 2), y, x, c),
        dev(z + 2 - 4 * lax.rem(lax.div(z, 2), 2), y, x, c),
        dev(mod(z + 4, NZ), y, x, c),
    )
    col_peers = (
        dev(z, y, x + 1 - 2 * lax.rem(x, 2), c),
        dev(z, y, mod(x + 2, NX), c),
        dev(z, y + 1 - 2 * lax.rem(y, 2), x, c),
        dev(z, mod(y + 2, NY), x, c),
    )

    barrier = pltpu.get_barrier_semaphore()
    row_steps = [(dz, dc) for dz in (4, 3, 5, 2, 6, 1, 7, 0) for dc in (0, 1) if dz or dc]
    col_steps = [(dy, dx) for dy in (2, 1, 3, 0) for dx in (2, 1, 3, 0) if dy or dx]

    def core_of(dc):
        return other if dc else c

    for peer in (zdev(1), zdev(-1), ydev(1), ydev(-1), xdev(1), xdev(-1), sibling):
        pl.semaphore_signal(barrier, inc=1, device_id=peer, device_id_type=MESH)
    b_all[z, c] = buyers_ref[...].astype(BF16)
    s_all[y, x] = sellers_ref[...].astype(BF16)
    own_pos = pos_ref[...] - market * (ROWS * NX * NC)
    pos_f[c] = jnp.broadcast_to(own_pos.astype(F32), (8, ROWS))
    pl.semaphore_wait(barrier, 7)

    names = {}
    landed = set()
    pending = []

    def sem_of(name):
        return names.setdefault(name, len(names))

    def send(name, src, dst, device):
        place = sem_of(name)
        copy = pltpu.make_async_remote_copy(
            src_ref=src, dst_ref=dst, send_sem=send_sem.at[place], recv_sem=recv_sem.at[place],
            device_id=device, device_id_type=MESH,
        )
        copy.start()
        pending.append(copy)

    def arrive(name, dst):
        place = sem_of(name)
        pltpu.make_async_remote_copy(
            src_ref=dst, dst_ref=dst, send_sem=send_sem.at[place], recv_sem=recv_sem.at[place],
            device_id=sibling, device_id_type=MESH,
        ).wait_recv()

    def need(name, dst):
        if name not in landed:
            landed.add(name)
            arrive(name, dst)

    def b_at(step, core, lo=0, rows=ROWS):
        return b_all.at[mod(z + step, NZ), core, pl.ds(lo, rows)]

    def s_at(first_axis, first_step, second_step, lo, rows):
        if first_axis == "x":
            return s_all.at[mod(y + second_step, NY), mod(x + first_step, NX), pl.ds(lo, rows)]
        return s_all.at[mod(y + first_step, NY), mod(x + second_step, NX), pl.ds(lo, rows)]

    halves = (("x", xdev, ydev, 0), ("y", ydev, xdev, 64))

    z_parts = {1: ((0, 32), (32, 32), (64, 64)), -1: ((96, 32), (64, 32), (0, 64))}

    def z_ref(hop, sign, i):
        lo, rows = z_parts[sign][i]
        return b_at(-hop * sign, c, lo, rows)

    def have(step):
        if abs(step) == 4:
            wanted = [(4, sign, i) for sign in (1, -1) for i in range(2)]
        else:
            wanted = [(abs(step), -1 if step > 0 else 1, i) for i in range(3)] if step else []
        for hop, sign, i in wanted:
            need(("b", hop, sign, i), z_ref(hop, sign, i))

    def s_ref(kind, h, step1, sign):
        axis, dev1, dev2, lo = halves[h]
        part = lo if sign == 1 else lo + 32
        if kind == "s0":
            return s_at(axis, -sign, 0, lo, 64)
        if kind == "s1":
            return s_at(axis, 2, 0, part, 32)
        if kind == "s2":
            return s_at(axis, step1, -sign, lo, 64)
        return s_at(axis, step1, 2, part, 32)

    def gather_step(kind, *key):
        if kind == "b":
            hop, sign, i = key
            ref = z_ref(hop, sign, i)
            if hop:
                need(("b", hop, sign, i), ref)
            send(("b", hop + 1, sign, i), ref, ref, zdev(sign))
        elif kind == "bs":
            step = key[0]
            have(step)
            send(("bs", step), b_at(step, c), b_at(step, c), sibling)
        elif kind == "flip":
            step, theirs = key
            if theirs:
                need(("bs", step), b_at(step, other))
            else:
                have(step)
            flip(step, other if theirs else c)
        elif kind == "s0" or kind == "s1":
            h, sign = key
            axis, dev1, dev2, lo = halves[h]
            if kind == "s0":
                ref = s_at(axis, 0, 0, lo, 64)
            else:
                need(("s0", h, sign), s_ref("s0", h, 0, sign))
                ref = s_at(axis, -sign, 0, lo if sign == 1 else lo + 32, 32)
            send((kind, h, sign), ref, ref, dev1(sign))
        else:
            h, step1, sign = key
            axis, dev1, dev2, lo = halves[h]
            if kind == "s2":
                if abs(step1) == 1:
                    need(("s0", h, -step1), s_ref("s0", h, 0, -step1))
                elif step1 == 2:
                    for way in (1, -1):
                        need(("s1", h, way), s_ref("s1", h, 0, way))
                ref = s_at(axis, step1, 0, lo, 64)
            elif kind == "s3":
                need(("s2", h, step1, sign), s_ref("s2", h, step1, sign))
                ref = s_at(axis, step1, -sign, lo if sign == 1 else lo + 32, 32)
            else:
                need(("s3", h, step1, sign), s_ref("s3", h, step1, sign))
                return
            send((kind, h, step1, sign), ref, ref, dev2(sign))

    def flip(step, core):
        zz = mod(z + step, NZ)
        bt_all[zz, core] = b_all[zz, core].T

    early = 8
    for task in GATHER_ORDER[:early]:
        gather_step(*task)
    send(("pos",), pos_f.at[c], pos_f.at[c], sibling)

    own_block = z * NY + y

    def eligible(block):
        return elig_ref[lax.div(block, NY) * NY + y, z * NY + lax.rem(block, NY)] > 0

    if not dense:

        def walk_back(i, following):
            block = NZ * NY - 1 - i
            next_ref[block] = following
            live = jnp.logical_and(eligible(block), block != own_block)
            return jnp.where(live, block, following)

        first = lax.fori_loop(0, NZ * NY, walk_back, own_block)

        def rank(block, seen):
            live = jnp.logical_and(eligible(block), block != own_block)
            slot_ref[block] = jnp.where(block == own_block, 0, jnp.where(live, 1 + seen, slots))
            return seen + jnp.where(live, 1, 0)

        lax.fori_loop(0, NZ * NY, rank, 0)
        list_ref[0] = own_block

        def walk(t, block):
            list_ref[t] = block
            return next_ref[block]

        lax.fori_loop(1, slots, walk, first)

    for task in GATHER_ORDER[early:]:
        gather_step(*task)
    arrive(("pos",), pos_f.at[other])

    eye = lax.broadcasted_iota(jnp.int32, (ROWS, ROWS), 0) == lax.broadcasted_iota(
        jnp.int32, (ROWS, ROWS), 1
    )
    unit = LOG2E / math.sqrt(EMBED)

    for core in range(NC):
        pos_cols[core * ROWS : (core + 1) * ROWS, :] = jnp.broadcast_to(
            as_column(pos_f[core, 0:1, :], eye), (ROWS, ROWS)
        )

    def hits(xx):
        lane = lax.broadcasted_iota(jnp.int32, (NC * ROWS, ROWS), 1) + (xx * NC + c) * ROWS
        return pos_cols[...] == lane.astype(F32)

    if not dense:
        row_stat[slots] = jnp.zeros((8, ROWS), F32)
        row_stat[slots, 0:2, :] = jnp.full((2, ROWS), neg_fill, F32)
        col_stat[slots] = jnp.zeros((8, ROWS), F32)
        col_stat[slots, 0:4, :] = jnp.full((4, ROWS), neg_fill, F32)

    def block_of(t):
        return t if dense else list_ref[t]

    def slot_of(zz, yy):
        return zz * NY + yy if dense else slot_ref[zz * NY + yy]

    def first_pass(t, carry):
        block = block_of(t)
        left = b_all[lax.div(block, NY)].reshape(NC * ROWS, EMBED)
        right = s_all[lax.rem(block, NY)].reshape(NX * ROWS, EMBED)
        tile = (
            lax.dot_general(left, right, (((1,), (1,)), ((), ())), preferred_element_type=F32)
            * unit
        )
        if dense:
            tile = jnp.where(eligible(block), tile, neg_fill)
        score[t] = tile
        row_top = jnp.max(tile, axis=1, keepdims=True)
        row_sum = jnp.sum(jnp.exp2(tile - row_top), axis=1, keepdims=True)
        col_top = jnp.max(tile, axis=0, keepdims=True)
        col_sum = jnp.sum(jnp.exp2(tile - col_top), axis=0, keepdims=True)
        for core in range(NC):
            span = slice(core * ROWS, (core + 1) * ROWS)
            row_stat[t, core : core + 1, :] = as_row(row_top[span], eye)
            row_stat[t, 2 + core : 3 + core, :] = as_row(row_sum[span], eye)
        for xx in range(NX):
            span = slice(xx * ROWS, (xx + 1) * ROWS)
            col_stat[t, xx : xx + 1, :] = col_top[:, span]
            col_stat[t, 4 + xx : 5 + xx, :] = col_sum[:, span]
        return carry

    def first_pair(i, carry):
        first_pass(2 * i, 0)
        first_pass(2 * i + 1, 0)
        return carry

    lax.fori_loop(0, slots // 2, first_pair, 0)
    own_slot = own_block if dense else 0
    matched = jnp.zeros((NC * ROWS, 1), F32)
    for xx in range(NX):
        matched = matched + jnp.sum(
            jnp.where(hits(xx), score[own_slot, :, xx * ROWS : (xx + 1) * ROWS], 0.0),
            axis=1, keepdims=True,
        )

    def merge(tops, sums):
        top = tops[0]
        for item in tops[1:]:
            top = jnp.maximum(top, item)
        total = jnp.zeros_like(top)
        for item, amount in zip(tops, sums):
            total = total + amount * jnp.exp2(item - top)
        return top, total

    for zz in range(NZ):
        stats = [row_stat[slot_of(zz, yy)] for yy in range(NY)]
        top, total = merge([a[0:2] for a in stats], [a[2:4] for a in stats])
        row_x[NC * zz : NC * zz + NC, :] = top + jnp.log2(total)
    for yy in range(NY):
        stats = [col_stat[slot_of(zz, yy)] for zz in range(NZ)]
        top, total = merge([a[0:4] for a in stats], [a[4:8] for a in stats])
        col_x[NX * yy : NX * yy + NX, :] = top + jnp.log2(total)
    row_x[16:24, :] = jnp.broadcast_to(jnp.sum(matched, axis=0, keepdims=True), (8, ROWS))

    for (dz, dc), (dy, dx) in zip(row_steps, col_steps):
        to = dev(mod(z + dz, NZ), y, x, core_of(dc))
        send(("row", dz, dc), row_x, row_in.at[z * NC + c], to)
        to = dev(z, mod(y + dy, NY), mod(x + dx, NX), c)
        send(("col", dy, dx), col_x, col_in.at[y * NX + x], to)
    row_in[z * NC + c] = row_x[...]
    col_in[y * NX + x] = col_x[...]
    for (dz, dc), (dy, dx) in reversed(list(zip(row_steps, col_steps))):
        arrive(("row", dz, dc), row_in.at[mod(z - dz, NZ) * NC + core_of(dc)])
        arrive(("col", dy, dx), col_in.at[mod(y - dy, NY) * NX + mod(x - dx, NX)])

    def log_sum(parts):
        top, total = merge(parts, [1.0] * len(parts))
        return top + jnp.log2(total)

    row_part = log_sum([row_in[i, 0:16, :] for i in range(16)])
    col_part = log_sum([col_in[i] for i in range(16)])
    matched_sum = row_in[0, 16:24, :]
    for i in range(1, 16):
        matched_sum = matched_sum + row_in[i, 16:24, :]
    row_lse[...] = row_part
    col_lse[...] = col_part
    line_terms = jnp.sum(jnp.sum(row_part, axis=1, keepdims=True), axis=0, keepdims=True)
    plane_terms = jnp.sum(jnp.sum(col_part, axis=1, keepdims=True), axis=0, keepdims=True)
    sum_x[0, 0] = jnp.broadcast_to(line_terms, (8, ROWS)) - 2.0 * matched_sum
    sum_x[0, 1] = jnp.broadcast_to(plane_terms, (8, ROWS))

    def loss_send(hop):
        send(("l0", hop), sum_x.at[hop, 0], sum_in.at[hop, 0], col_peers[hop])
        send(("l1", hop), sum_x.at[hop, 1], sum_in.at[hop, 1], row_peers[hop])

    def loss_add(hop):
        arrive(("l0", hop), sum_in.at[hop, 0])
        arrive(("l1", hop), sum_in.at[hop, 1])
        sum_x[hop + 1] = sum_x[hop] + sum_in[hop]

    for zz in range(NZ):
        for core in range(NC):
            place = zz * NC + core
            rl_cols[zz, core * ROWS : (core + 1) * ROWS, :] = jnp.broadcast_to(
                as_column(row_lse[place : place + 1, :], eye) + 1.0, (ROWS, ROWS)
            )

    def second_pass(t, own):
        block = block_of(t)
        zz, yy = lax.div(block, NY), lax.rem(block, NY)
        row_part = rl_cols[zz]
        parts = []
        for xx in range(NX):
            tile = score[t, :, xx * ROWS : (xx + 1) * ROWS]
            col_part = col_lse[pl.ds(yy * NX + xx, 1), :] + 1.0
            mixed = jnp.exp2(tile - row_part) + jnp.exp2(tile - col_part)
            if dense:
                mixed = mixed - jnp.where(block == own_block, jnp.where(hits(xx), 1.0, 0.0), 0.0)
            elif own:
                mixed = mixed - jnp.where(hits(xx), 1.0, 0.0)
            parts.append(mixed.astype(BF16))
        weights = jnp.concatenate(parts, axis=1)
        right = s_all[yy].reshape(NX * ROWS, EMBED)
        term = jnp.dot(weights, right, preferred_element_type=F32)
        for core in range(NC):
            part = term[core * ROWS : (core + 1) * ROWS]
            if dense:
                pbuf[zz, core] = pbuf[zz, core] + part
            else:
                pbuf[t, core] = part
        flipped = jnp.concatenate([bt_all[zz, 0], bt_all[zz, 1]], axis=1)
        term = jnp.dot(flipped, weights, preferred_element_type=F32)
        for xx in range(NX):
            part = term[:, xx * ROWS : (xx + 1) * ROWS]
            if dense:
                qbuf[yy, xx] = qbuf[yy, xx] + part
            else:
                qbuf[t, xx] = part

    def other_blocks(i, carry):
        second_pass(2 * i, False)
        second_pass(2 * i + 1, False)
        return carry

    loss_send(0)
    if dense:
        pbuf[...] = jnp.zeros(pbuf.shape, F32)
        qbuf[...] = jnp.zeros(qbuf.shape, F32)
        lax.fori_loop(0, slots // 2, other_blocks, 0)
    else:
        second_pass(0, True)
        second_pass(1, False)
        lax.fori_loop(1, slots // 2, other_blocks, 0)
        pbuf[slots] = jnp.zeros(pbuf.shape[1:], F32)
        qbuf[slots] = jnp.zeros(qbuf.shape[1:], F32)
    step_rows = 32

    def by_rows(lo, rows, body):
        def at(i, carry):
            body(pl.multiple_of(lo + i * step_rows, step_rows))
            return carry

        lax.fori_loop(0, rows // step_rows, at, 0)

    def p_sum(zz, core, at):
        if dense:
            return pbuf[zz, core, pl.ds(at, step_rows), :]
        total = None
        for yy in range(NY):
            term = pbuf[slot_of(zz, yy), core, pl.ds(at, step_rows), :]
            total = term if total is None else total + term
        return total

    def q_sum(yy, xx, at):
        if dense:
            return qbuf[yy, xx, pl.ds(at, step_rows), :]
        total = None
        for zz in range(NZ):
            term = qbuf[slot_of(zz, yy), xx, pl.ds(at, step_rows), :]
            total = term if total is None else total + term
        return total

    def to_f32(ref, place, at):
        return ref[(*place, pl.ds(at, step_rows))].astype(F32)

    order = (4, 3, -3, 2, -2, 1, -1, 0)

    def sib_send(place):
        def fill(at):
            value = p_sum(mod(z + order[place], NZ), other, at)
            sib_s[place, pl.ds(at, step_rows), :] = value.astype(BF16)

        by_rows(0, ROWS, fill)
        send(("gs", place), sib_s.at[place], sib_r.at[place], sibling)

    def z_value(place, at):
        return p_sum(mod(z + order[place], NZ), c, at) + to_f32(sib_r, (place,), at)

    z_places = ((0, 1, 3, 5), (0, 2, 4, 6))

    def z_send(d, hop, i):
        sign, lo, place = 1 - 2 * d, 32 * i, z_places[d][hop]
        started = hop == 0 or (hop == 1 and (lo < 64) == (d == 1))
        need(("gs", place), sib_r.at[place])
        if not started:
            arrive(("gz", d, hop - 1, i), z_r.at[d, hop - 1, pl.ds(lo, 32)])
        value = z_value(place, lo)
        if not started:
            value = value + to_f32(z_r, (d, hop - 1,), lo)
        z_s[d, hop, pl.ds(lo, 32), :] = value.astype(BF16)
        part = pl.ds(lo, 32)
        send(("gz", d, hop, i), z_s.at[d, hop, part], z_r.at[d, hop, part], zdev(sign))

    grads = (("y", ydev, xdev, 0, x), ("x", xdev, ydev, 256, y))
    offsets = (2, 1, -1, 0)
    groups = ((0,), (1, 2), (3,))

    def q_at(axis, step, lane, at):
        if axis == "y":
            return q_sum(mod(y + step, NY), lane, at)
        return q_sum(lane, mod(x + step, NX), at)

    def f_send(kind, h, d, g):
        axis, dev1, dev2, base, place = grads[h]
        sign = 1 - 2 * d
        group = groups[g]
        part = pl.ds(group[0], len(group))
        half = 1 - d if kind == "fa" else d
        if kind == "fb":
            arrive(("f0", h, d, g), f0_r.at[h, d, part])
        for k in group:
            def fill(at):
                step = 2 if kind == "f0" else sign
                value = q_at(axis, step, mod(place + offsets[k], 4), base + half * 128 + at)
                if kind == "f0":
                    f0_s[h, d, k, pl.ds(at, step_rows), :] = value.astype(BF16)
                    return
                if kind == "fb":
                    value = value + to_f32(f0_r, (h, d, k,), at)
                f1_s[h, d, half, k, pl.ds(at, step_rows), :] = value.astype(BF16)

            by_rows(0, 128, fill)
        if kind == "f0":
            send((kind, h, d, g), f0_s.at[h, d, part], f0_r.at[h, d, part], dev1(sign))
        else:
            send((kind, h, d, g), f1_s.at[h, d, half, part], f1_r.at[h, d, half, part], dev1(sign))

    def mid_sum(h, g):
        axis, dev1, dev2, base, place = grads[h]
        group = groups[g]
        part = pl.ds(group[0], len(group))
        for d in range(2):
            arrive(("fa", h, d, g), f1_r.at[h, d, 1 - d, part])
            arrive(("fb", h, d, g), f1_r.at[h, d, d, part])
        for k in group:
            for half in range(2):
                def fill(at):
                    value = q_at(axis, 0, mod(place + offsets[k], 4), base + half * 128 + at)
                    value = value + to_f32(f1_r, (h, 0, half, k,), at)
                    value = value + to_f32(f1_r, (h, 1, half, k,), at)
                    mid[h, k, pl.ds(half * 128 + at, step_rows), :] = value

                by_rows(0, 128, fill)

    def g_send(kind, h, d):
        axis, dev1, dev2, base, place = grads[h]
        sign = 1 - 2 * d
        far_lo, near_lo = d * 128, 128 - d * 128
        if kind == "g0":
            g0_s[h, d] = mid[h, 0, far_lo : far_lo + 128, :].astype(BF16)
            send(("g0", h, d), g0_s.at[h, d], g0_r.at[h, d], dev2(sign))
            return
        arrive(("g0", h, d), g0_r.at[h, d])
        g1_s[h, d, near_lo : near_lo + 128, :] = mid[h, 1 + d, near_lo : near_lo + 128, :].astype(BF16)
        g1_s[h, d, far_lo : far_lo + 128, :] = (
            mid[h, 1 + d, far_lo : far_lo + 128, :] + g0_r[h, d].astype(F32)
        ).astype(BF16)
        send(("g1", h, d), g1_s.at[h, d], g1_r.at[h, d], dev2(sign))

    def g_end(h):
        for d in range(2):
            arrive(("g1", h, d), g1_r.at[h, d])
        seller_t[h * 256 : (h + 1) * 256, :] = (
            mid[h, 3] + g1_r[h, 0].astype(F32) + g1_r[h, 1].astype(F32)
        )

    def z_end():
        need(("gs", 7), sib_r.at[7])
        for d in range(2):
            for i in range(4):
                arrive(("gz", d, 3, i), z_r.at[d, 3, pl.ds(32 * i, 32)])

        def finish(at):
            bgrad_ref[pl.ds(at, step_rows), :] = (
                z_value(7, at) + to_f32(z_r, (0, 3,), at) + to_f32(z_r, (1, 3,), at)
            )

        by_rows(0, ROWS, finish)

    def loss_step(hop):
        loss_add(hop)
        if hop < 3:
            loss_send(hop + 1)

    actions = {
        "sib": sib_send, "z": z_send, "zend": z_end, "mid": mid_sum, "gend": g_end, "loss": loss_step,
    }
    for task in RETURN_ORDER:
        if task[0] in actions:
            actions[task[0]](*task[1:])
        elif task[0] in ("g0", "g1"):
            g_send(*task)
        else:
            f_send(*task)
    sgrad_ref[...] = seller_t[...].T
    loss_ref[...] = (sum_x[4, 0, 0:1, :] + sum_x[4, 1, 0:1, :]) * (
        math.log(2.0) / (2.0 * ROWS * NZ * NY * NX * NC)
    )
    for copy in pending:
        copy.wait_send()


def vmem(shape, dtype):
    return pltpu.VMEM(shape, dtype)


def fused(dense, slots, buyers, sellers, eligibility, positives):
    extra = 0 if dense else 1
    scratch = [
        vmem((NZ, NC, ROWS, EMBED), BF16),
        vmem((NY, NX, ROWS, EMBED), BF16),
        vmem((NZ, NC, EMBED, ROWS), BF16),
        vmem((slots, NC * ROWS, NX * ROWS), F32),
        vmem((NZ if dense else slots + 1, NC, ROWS, EMBED), F32),
        vmem((NY if dense else slots + 1, NX, EMBED, ROWS), F32),
        vmem((NC, 8, ROWS), F32),
        vmem((NC * ROWS, ROWS), F32),
        vmem((slots + extra, 8, ROWS), F32),
        vmem((slots + extra, 8, ROWS), F32),
        vmem((24, ROWS), F32),
        vmem((16, 24, ROWS), F32),
        vmem((16, ROWS), F32),
        vmem((16, 16, ROWS), F32),
        vmem((16, ROWS), F32),
        vmem((16, ROWS), F32),
        vmem((5, 2, 8, ROWS), F32),
        vmem((4, 2, 8, ROWS), F32),
        vmem((NZ, NC * ROWS, ROWS), F32),
        vmem((NZ, ROWS, EMBED), BF16),
        vmem((NZ, ROWS, EMBED), BF16),
        vmem((2, 4, ROWS, EMBED), BF16),
        vmem((2, 4, ROWS, EMBED), BF16),
        vmem((2, 2, 4, 128, ROWS), BF16),
        vmem((2, 2, 4, 128, ROWS), BF16),
        vmem((2, 2, 2, 4, 128, ROWS), BF16),
        vmem((2, 2, 2, 4, 128, ROWS), BF16),
        vmem((2, 4, 256, ROWS), F32),
        vmem((2, 2, 128, ROWS), BF16),
        vmem((2, 2, 128, ROWS), BF16),
        vmem((2, 2, 256, ROWS), BF16),
        vmem((2, 2, 256, ROWS), BF16),
        vmem((EMBED, ROWS), F32),
        pltpu.SMEM((NZ * NY,), jnp.int32),
        pltpu.SMEM((NZ * NY,), jnp.int32),
        pltpu.SMEM((slots,), jnp.int32),
        pltpu.SemaphoreType.DMA((224,)),
        pltpu.SemaphoreType.DMA((224,)),
    ]
    in_vmem = pl.BlockSpec(memory_space=pltpu.VMEM)
    buyer_grad, seller_grad, loss = pl.pallas_call(
        functools.partial(kernel, dense),
        out_shape=(
            jax.ShapeDtypeStruct((ROWS, EMBED), F32),
            jax.ShapeDtypeStruct((ROWS, EMBED), F32),
            jax.ShapeDtypeStruct((1, ROWS), F32),
        ),
        in_specs=[in_vmem, in_vmem, pl.BlockSpec(memory_space=pltpu.SMEM), in_vmem],
        out_specs=(in_vmem, in_vmem, in_vmem),
        scratch_shapes=scratch,
        compiler_params=pltpu.CompilerParams(
            collective_id=1 if dense else 0, has_side_effects=True, vmem_limit_bytes=60 * 1024 * 1024
        ),
        name="two_tower_dense" if dense else "two_tower",
    )(buyers, sellers, eligibility, positives.reshape(1, ROWS))
    return (buyer_grad, seller_grad, loss[0, 0])


def shards(buyers, sellers, eligibility, positives):
    blocks = (eligibility > 0).astype(jnp.int32).reshape(NZ, NY, NZ, NY)
    busiest = jnp.max(jnp.sum(blocks, axis=(0, 3)))
    return lax.cond(
        busiest <= SLOTS,
        functools.partial(fused, False, SLOTS),
        functools.partial(fused, True, NZ * NY),
        buyers, sellers, eligibility, positives,
    )


def solution(mesh):
    return jax.shard_map(
        shards,
        mesh=mesh,
        in_specs=(
            P(("market", "sub"), None),
            P(("market", "sub"), None),
            P(),
            P(("market", "sub")),
        ),
        out_specs=(P(("market", "sub"), None), P(("market", "sub"), None), P()),
        check_vma=False,
    )
```
